512 devices in a mesh: var: 2 (over core), tok: 4 (over x), wide: 64 (over y, z).
Axes of the slice: x: 4, y: 8, z: 8, core: 2. Of those that a mesh axis runs over, the one named last changes fastest.
Arguments:
- tokens: bfloat16 [512, 8192], P('wide', 'tok'), may hold values from -8 to 8
- norm_gain: float32 [8192], P('tok'), may hold values from 0 to 2
- gate_parent: bfloat16 [8192, 20480], P('tok', 'wide'), may hold values from -0.0625 to 0.0625
- up_parent: bfloat16 [8192, 20480], P('tok', 'wide'), may hold values from -1 to 1
- down_parent: bfloat16 [20480, 8192], P('wide', 'tok'), may hold values from -1 to 1
- kept: int32 [2, 10240], P('var'), may hold values from 0 to 20479, as said below
Outputs:
- loss: float32 [2], P('var')
- grad_down: bfloat16 [2, 10240, 8192], P('var', 'wide', 'tok')
The draws below stay inside these ranges and needn't reach their ends.
Inputs may be any that keep to these rules, and one draw needn't show every extreme that they name: Each row is ascending and distinct. Entries 2 * 160 * m to 2 * 160 * (m + 1) - 1 of a row are units of parent blocks 2m and 2m+1 (parent block b holds units b * 320 to (b + 1) * 320 - 1); each parent block holds between 80 and 240 kept units of a row, and both ends are reached in every row.
All inputs are finite; a program needn't handle non-finite values.
Results may differ from the reference program's by a relative error of at most 0.0059.
Values may be sent and summed in bfloat16 or wider, within the bound.
No kernel may reach another device: no remote copies, remote signals or barrier semaphores. Data moves between devices by JAX's collectives and lax.ppermute only.
A program may use at most 64 MiB of HBM per device.

```python
import math
import jax
import jax.numpy as jnp
from jax import lax

D = 8192
FF = 20480
TOKENS = 512
KEEP = 10240
VARIANTS = 2
LOCAL = 320
BLOCK = 160
PAIRS = 32


def column_classes(key):
    return jax.random.randint(jax.random.fold_in(key, 501), (D,), 0, 2).astype(jnp.float32)


def unit_signs(key):
    return 2.0 * jax.random.randint(jax.random.fold_in(key, 502), (FF,), 0, 2).astype(jnp.float32) - 1.0


def base_values(key, shape):
    return jax.random.truncated_normal(key, -4.0, 4.0, shape, jnp.float32)


def draw_tokens(key, part):
    classes = column_classes(key)
    key = jax.random.fold_in(key, 21)
    first, second, third = jax.random.split(key, 3)
    rows = jnp.arange(TOKENS, dtype=jnp.float32)
    trend = 0.15 + 0.7 * rows / (TOKENS - 1)
    groups = jax.random.uniform(first, (TOKENS // 8,), jnp.float32, -0.15, 0.15)
    jitter = jax.random.uniform(second, (TOKENS,), jnp.float32, -0.05, 0.05)
    share = jnp.clip(trend + jnp.repeat(groups, 8) + jitter, 0.05, 0.95)
    values = base_values(third, (TOKENS, D))
    amplitude = jnp.where(classes[None, :] > 0.5, jnp.sqrt(2.0 * share)[:, None], jnp.sqrt(2.0 * (1.0 - share))[:, None])
    return (values * amplitude).astype(jnp.bfloat16)


def draw_norm_gain(key, part):
    classes = column_classes(key)
    key = jax.random.fold_in(key, 22)
    spread = jax.random.uniform(key, (D,), jnp.float32, 0.0, 1.0)
    return jnp.where(classes > 0.5, 1.3 + 0.7 * spread, 0.3 + 0.2 * spread).astype(jnp.float32)


def draw_up_parent(key, part):
    signs = unit_signs(key)
    key = jax.random.fold_in(key, 23)
    first, second = jax.random.split(key, 2)
    values = base_values(first, (D, FF))
    common = jax.random.truncated_normal(second, -4.0, 4.0, (D,), jnp.float32)
    return ((values + 0.4 * signs[None, :] * common[:, None]) / math.sqrt(D)).astype(jnp.bfloat16)


def draw_down_parent(key, part):
    signs = unit_signs(key)
    key = jax.random.fold_in(key, 24)
    first, second = jax.random.split(key, 2)
    values = base_values(first, (FF, D))
    common = jax.random.truncated_normal(second, -4.0, 4.0, (D,), jnp.float32)
    strength = 7.2 / math.sqrt(FF)
    return ((values + strength * signs[:, None] * common[None, :]) / math.sqrt(FF)).astype(jnp.bfloat16)


def draw_kept(key, part):
    key = jax.random.fold_in(key, 11)
    first, second, third, fourth = jax.random.split(key, 4)
    lowest = BLOCK // 2
    highest = 3 * BLOCK // 2
    counts_even = jax.random.randint(first, (VARIANTS, PAIRS), lowest, highest + 1)
    top_pair = jax.random.randint(second, (VARIANTS,), 0, PAIRS)
    offset = jax.random.randint(third, (VARIANTS,), 1, max(PAIRS, 2))
    low_pair = (top_pair + offset) % PAIRS
    positions = jnp.arange(PAIRS, dtype=jnp.int32)[None, :]
    counts_even = jnp.where(positions == low_pair[:, None], lowest, counts_even)
    counts_even = jnp.where(positions == top_pair[:, None], highest, counts_even)
    counts = jnp.stack([counts_even, 2 * BLOCK - counts_even], axis=2).reshape(VARIANTS, 2 * PAIRS)
    scores = jax.random.randint(fourth, (VARIANTS, 2 * PAIRS, LOCAL), 0, 1 << 20)
    scores = scores * LOCAL + jnp.arange(LOCAL, dtype=jnp.int32)[None, None, :]
    order = jnp.argsort(scores, axis=2)
    ranks = jnp.argsort(order, axis=2)
    chosen = (ranks < counts[:, :, None]).reshape(VARIANTS, FF)
    return jax.vmap(lambda row: jnp.nonzero(row, size=KEEP)[0])(chosen).astype(jnp.int32)


def block_levels(own_key, dims, cuts, least, largest):
    gain, own = 1.0, jax.random.fold_in(own_key, 6)
    for dim, parts in cuts:
        steps = jnp.exp(jax.random.uniform(jax.random.fold_in(own, dim), (parts,), jnp.float32, least / len(cuts), largest / len(cuts)))
        gain = gain * jnp.repeat(steps, dims[dim] // parts).reshape([-1 if axis == dim else 1 for axis in range(len(dims))])
    return gain


def gaussian(stream_key, shape, deviation, bound, shards=(), kind=jnp.bfloat16):
    entries = jax.random.normal(stream_key, shape, jnp.float32) * deviation
    if len(shards) > 0:
        entries = block_levels(stream_key, shape, shards, -0.22, 0.18) * entries
    return jnp.clip(entries, min=-bound, max=bound).astype(kind)


def setup_inputs(seed: int = 0) -> dict:
    key_list = jax.random.split(jax.random.key(seed), 7)
    return {
        "tokens": draw_tokens(jax.random.fold_in(key_list[6], 71), 0),
        "norm_gain": draw_norm_gain(jax.random.fold_in(key_list[6], 71), 0),
        "gate_parent": gaussian(key_list[2], (D, FF), D ** -0.5, 0.0625, ((0, 4), (1, 64))),
        "up_parent": draw_up_parent(jax.random.fold_in(key_list[6], 71), 0),
        "down_parent": draw_down_parent(jax.random.fold_in(key_list[6], 71), 0),
        "kept": draw_kept(jax.random.fold_in(key_list[6], 71), 0),
    }


def reference(tokens, norm_gain, gate_parent, up_parent, down_parent, kept):
    widths = tokens.astype(jnp.float32)
    scaled = lax.rsqrt(lax.optimization_barrier(jnp.mean(widths * widths, axis=1, keepdims=True)) + 1e-05)
    normed = (widths * scaled * norm_gain[None, :]).astype(jnp.bfloat16)
    gate = jnp.dot(normed, gate_parent, preferred_element_type=jnp.float32)
    up = jnp.dot(normed, up_parent, preferred_element_type=jnp.float32)
    hidden = (jax.nn.silu(gate) * up).astype(jnp.bfloat16)
    factor = 1.0 / math.sqrt(TOKENS)
    losses = []
    grads = []
    for variant in range(VARIANTS):
        chosen = kept[variant].astype(jnp.int32)
        keepmask = jnp.zeros((FF,), jnp.bool_).at[chosen].set(True)
        dropped = jnp.where(keepmask[None, :], jnp.zeros((), jnp.bfloat16), hidden)
        residual = -jnp.dot(dropped, down_parent, preferred_element_type=jnp.float32)
        losses.append(jnp.mean(residual * residual))
        rounded = residual.astype(jnp.bfloat16)
        columns = jnp.take(hidden, chosen, axis=1)
        product = lax.dot_general(columns, rounded, (((0,), (0,)), ((), ())), preferred_element_type=jnp.float32)
        grads.append((product * factor).astype(jnp.bfloat16))
    return (jnp.stack(losses), jnp.stack(grads))
```

```python
import math

import jax
import jax.numpy as jnp
from jax import lax
from jax.sharding import PartitionSpec as P

D = 8192
SIDE = 8


def block_groups():
    return [
        [(2 * a + i) * SIDE + 2 * b + j for i in range(2) for j in range(2)]
        for a in range(SIDE // 2)
        for b in range(SIDE // 2)
    ]


def stride_groups():
    return [
        [(2 * a + i) * SIDE + 2 * b + j for a in range(SIDE // 2) for b in range(SIDE // 2)]
        for i in range(2)
        for j in range(2)
    ]


def spread(shard, count, axes, groups=None):
    stacked = jnp.broadcast_to(shard[None], (count,) + shard.shape)
    return lax.all_to_all(stacked, axes, 0, 0, axis_index_groups=groups)


def hi_lo(value):
    hi = lax.reduce_precision(value, 8, 7)
    return hi.astype(jnp.bfloat16), (value - hi).astype(jnp.bfloat16)


def per_device(tokens, norm_gain, gate_parent, up_parent, down_parent, kept):
    n_wide = lax.axis_size("wide")
    n_tok = lax.axis_size("tok")
    core = lax.axis_index("var")
    wide = lax.axis_index("wide")
    row, col = wide // SIDE, wide % SIDE
    slot = (row % 2) * 2 + col % 2
    local = gate_parent.shape[1]
    width = tokens.shape[1]
    blocks = block_groups()

    half = tokens.shape[0] // 2
    mine = lax.dynamic_slice_in_dim(tokens, core * half, half, 0)
    gathered = spread(mine, n_wide, "wide").reshape(n_wide * half, width)

    quarter = down_parent.shape[1] // 4
    gathered, down = lax.optimization_barrier((gathered, down_parent))
    down_block = jnp.zeros((4, local, quarter), jnp.bfloat16)
    own = lax.dynamic_slice_in_dim(down, slot * quarter, quarter, 1)
    down_block = lax.dynamic_update_slice_in_dim(down_block, own[None], slot, 0)
    for k in range(1, 4):
        perm = [(w, w ^ ((k // 2) * SIDE + k % 2)) for w in range(n_wide)]
        piece = lax.dynamic_slice_in_dim(down, (slot ^ k) * quarter, quarter, 1)
        piece = lax.ppermute(piece, "wide", perm)
        down_block = lax.dynamic_update_slice_in_dim(down_block, piece[None], slot ^ k, 0)
    down_block = down_block.reshape(4 * local, quarter)

    widths = gathered.astype(jnp.float32)
    squares = jnp.sum(widths * widths, axis=1)
    gained = (widths * norm_gain[None, :]).astype(jnp.bfloat16)
    sq_hi, sq_lo = hi_lo(squares)
    lanes = lax.broadcasted_iota(jnp.int32, (n_wide * half, 128), 1)
    extra = jnp.where(lanes == 0, sq_hi[:, None], jnp.where(lanes == 1, sq_lo[:, None], jnp.zeros((), jnp.bfloat16)))
    partial = jnp.concatenate(
        [
            jnp.dot(gained, gate_parent, preferred_element_type=jnp.float32).astype(jnp.bfloat16),
            jnp.dot(gained, up_parent, preferred_element_type=jnp.float32).astype(jnp.bfloat16),
            extra,
        ],
        axis=1,
    )
    rows = n_wide * half // n_tok
    scattered = lax.all_to_all(partial.reshape(n_tok, rows, 2 * local + 128), "tok", 0, 0)
    total = jnp.sum(scattered.astype(jnp.float32), axis=0)
    scale = lax.rsqrt((total[:, 2 * local] + total[:, 2 * local + 1]) / D + 1e-05)[:, None]
    gate = total[:, :local] * scale
    up = total[:, local : 2 * local] * scale
    hidden = (jax.nn.silu(gate) * up).astype(jnp.bfloat16)

    groups = [[t * n_wide + w for t in range(n_tok) for w in block] for block in blocks]
    hidden = spread(hidden, n_tok * 4, ("tok", "wide"), groups)
    hidden = spread(hidden, 2, "var").reshape(2, n_tok, 4, rows, local)
    total_rows = 2 * n_tok * rows
    hidden = hidden.transpose(0, 1, 3, 2, 4).reshape(total_rows, 4 * local)

    var_kept = kept[0]
    block = var_kept.shape[0] // n_wide
    selected = []
    masks = []
    for i in range(2):
        pair = (row // 2 * 2 + i) * (SIDE // 2) + col // 2
        names = lax.dynamic_slice_in_dim(var_kept, pair * 2 * block, 2 * block) - pair * 2 * local
        matches = jnp.arange(2 * local, dtype=jnp.int32)[:, None] == names[None, :]
        masks.append(jnp.any(matches, axis=1))
        units = hidden[:, i * 2 * local : (i + 1) * 2 * local]
        selected.append(
            jnp.dot(units, matches.astype(jnp.bfloat16), preferred_element_type=jnp.float32).astype(jnp.bfloat16)
        )
    dropped = jnp.where(jnp.concatenate(masks)[None, :], jnp.zeros((), jnp.bfloat16), hidden)
    share = -jnp.dot(dropped, down_block, preferred_element_type=jnp.float32)

    strides = stride_groups()
    n_blocks = n_wide // 4
    shares = share.astype(jnp.bfloat16).reshape(n_blocks, total_rows // n_blocks, quarter)
    shares = lax.all_to_all(shares, "wide", 0, 0, axis_index_groups=strides)
    piece = jnp.sum(shares.astype(jnp.float32), axis=0).astype(jnp.bfloat16)
    rounded = spread(piece, n_blocks, "wide", strides).reshape(total_rows, quarter)

    errors = rounded.astype(jnp.float32)
    error_sum = lax.psum(jnp.sum(errors * errors), "tok")
    err_hi, err_lo = hi_lo(error_sum)

    factor = 1.0 / math.sqrt(total_rows)
    contract = (((0,), (0,)), ((), ()))
    grads = [
        (lax.dot_general(s, rounded, contract, preferred_element_type=jnp.float32) * factor).astype(jnp.bfloat16)
        for s in selected
    ]
    grad = jnp.concatenate(grads, axis=0).reshape(4, block, quarter)
    lanes = lax.broadcasted_iota(jnp.int32, (4, 16, quarter), 2)
    extra = jnp.where(lanes == 0, err_hi, jnp.where(lanes == 1, err_lo, jnp.zeros((), jnp.bfloat16)))
    swapped = lax.all_to_all(jnp.concatenate([grad, extra], axis=1), "wide", 0, 0, axis_index_groups=blocks)
    grad = swapped[:, :block].transpose(1, 0, 2).reshape(block, 4 * quarter)
    loss = jnp.sum(swapped[:, block, :2].astype(jnp.float32)) / (total_rows * D)
    return (loss.reshape(1), grad[None])


def solution(mesh):
    in_specs = (
        P("wide", "tok"),
        P("tok"),
        P("tok", "wide"),
        P("tok", "wide"),
        P("wide", "tok"),
        P("var", None),
    )
    out_specs = (P("var"), P("var", "wide", "tok"))
    return jax.shard_map(
        per_device, mesh=mesh, in_specs=in_specs, out_specs=out_specs, check_vma=False
    )
```

```python
import functools
import math

import jax
import jax.numpy as jnp
from jax import lax
from jax.experimental import pallas as pl
from jax.experimental.pallas import tpu as pltpu
from jax.sharding import PartitionSpec as P

D = 8192
SIDE = 8


def block_groups():
    return [
        [(2 * a + i) * SIDE + 2 * b + j for i in range(2) for j in range(2)]
        for a in range(SIDE // 2)
        for b in range(SIDE // 2)
    ]


def stride_groups():
    return [
        [(2 * a + i) * SIDE + 2 * b + j for a in range(SIDE // 2) for b in range(SIDE // 2)]
        for i in range(2)
        for j in range(2)
    ]


def spread(shard, count, axes, groups=None):
    stacked = jnp.broadcast_to(shard[None], (count,) + shard.shape)
    return lax.all_to_all(stacked, axes, 0, 0, axis_index_groups=groups)


def hi_lo(value):
    hi = lax.reduce_precision(value, 8, 7)
    return hi.astype(jnp.bfloat16), (value - hi).astype(jnp.bfloat16)


VMEM = pl.BlockSpec(memory_space=pltpu.VMEM)
SMEM = pl.BlockSpec(memory_space=pltpu.SMEM)


def call(kernel, out_shape, in_specs, flops, size):
    out_specs = jax.tree.map(lambda _: VMEM, out_shape)
    return pl.pallas_call(
        kernel,
        out_shape=out_shape,
        in_specs=in_specs,
        out_specs=out_specs,
        compiler_params=pltpu.CompilerParams(vmem_limit_bytes=32 * 1024 * 1024),
        cost_estimate=pl.CostEstimate(flops=flops, bytes_accessed=size, transcendentals=0),
    )


def residual_kernel(slot_ref, hidden_ref, drop_ref, down0, down1, down2, down3, out_ref):
    slot = slot_ref[0]
    downs = (down0, down1, down2, down3)
    for core in range(2):
        total = None
        for k in range(4):
            index = slot ^ k
            units = hidden_ref[core, index] * drop_ref[index]
            term = jnp.dot(units, downs[k][...], preferred_element_type=jnp.float32)
            total = term if total is None else total + term
        out_ref[core] = (-total).astype(out_ref.dtype)


def select_kernel(names_ref, hidden_ref, out_ref):
    local = hidden_ref.shape[3]
    rows = hidden_ref.shape[2]
    count = names_ref.shape[1]
    for pair in range(2):
        names = names_ref[pair]
        for core in range(2):
            total = None
            for i in range(2):
                units = lax.broadcasted_iota(jnp.int32, (count, local), 1) + i * local
                picker = jnp.where(units == names, 1.0, 0.0).astype(jnp.bfloat16)
                term = lax.dot_general(
                    picker,
                    hidden_ref[core, 2 * pair + i],
                    (((1,), (1,)), ((), ())),
                    preferred_element_type=jnp.float32,
                )
                total = term if total is None else total + term
            out_ref[pair, :, core * rows : (core + 1) * rows] = total.astype(out_ref.dtype)


def gradient_kernel(factor, chosen_ref, rounded_ref, grad_ref, error_ref):
    rounded = rounded_ref[...]
    block = grad_ref.shape[1]
    for pair in range(2):
        product = jnp.dot(chosen_ref[pair], rounded, preferred_element_type=jnp.float32) * factor
        for i in range(2):
            grad_ref[2 * pair + i] = product[i * block : (i + 1) * block].astype(grad_ref.dtype)
    errors = rounded.astype(jnp.float32)
    columns = jnp.sum(errors * errors, axis=0, keepdims=True)
    total = columns[:, :128]
    for i in range(1, columns.shape[1] // 128):
        total = total + columns[:, i * 128 : (i + 1) * 128]
    error_ref[...] = total


def interleave_kernel(in_ref, out_ref):
    width = in_ref.shape[2]
    for i in range(in_ref.shape[0]):
        out_ref[:, i * width : (i + 1) * width] = in_ref[i]


def per_device(tokens, norm_gain, gate_parent, up_parent, down_parent, kept):
    n_wide = lax.axis_size("wide")
    n_tok = lax.axis_size("tok")
    core = lax.axis_index("var")
    wide = lax.axis_index("wide")
    row, col = wide // SIDE, wide % SIDE
    slot = (row % 2) * 2 + col % 2
    local = gate_parent.shape[1]
    width = tokens.shape[1]
    blocks = block_groups()

    half = tokens.shape[0] // 2
    mine = lax.dynamic_slice_in_dim(tokens, core * half, half, 0)
    gathered = spread(mine, n_wide, "wide").reshape(n_wide * half, width)

    widths = gathered.astype(jnp.float32)
    squares = jnp.sum(widths * widths, axis=1)
    gained = (widths * norm_gain[None, :]).astype(jnp.bfloat16)
    sq_hi, sq_lo = hi_lo(squares)
    lanes = lax.broadcasted_iota(jnp.int32, (n_wide * half, 128), 1)
    extra = jnp.where(lanes == 0, sq_hi[:, None], jnp.where(lanes == 1, sq_lo[:, None], jnp.zeros((), jnp.bfloat16)))
    partial = jnp.concatenate(
        [
            jnp.dot(gained, gate_parent, preferred_element_type=jnp.float32).astype(jnp.bfloat16),
            jnp.dot(gained, up_parent, preferred_element_type=jnp.float32).astype(jnp.bfloat16),
            extra,
        ],
        axis=1,
    )
    rows = n_wide * half // n_tok

    quarter = down_parent.shape[1] // 4
    partial, down = lax.optimization_barrier((partial, down_parent))
    downs = [lax.dynamic_slice_in_dim(down, (slot ^ k) * quarter, quarter, 1) for k in range(4)]
    for k in range(1, 4):
        perm = [(w, w ^ ((k // 2) * SIDE + k % 2)) for w in range(n_wide)]
        downs[k] = lax.ppermute(downs[k], "wide", perm)

    scattered = lax.all_to_all(partial.reshape(n_tok, rows, 2 * local + 128), "tok", 0, 0)
    scattered, *downs = lax.optimization_barrier((scattered, *downs))
    total = jnp.sum(scattered.astype(jnp.float32), axis=0)
    scale = lax.rsqrt((total[:, 2 * local] + total[:, 2 * local + 1]) / D + 1e-05)[:, None]
    gate = total[:, :local] * scale
    up = total[:, local : 2 * local] * scale
    hidden = (jax.nn.silu(gate) * up).astype(jnp.bfloat16)

    groups = [[t * n_wide + w for w in block for t in range(n_tok)] for block in blocks]
    hidden = spread(hidden, n_tok * 4, ("tok", "wide"), groups)
    hidden = spread(hidden, 2, "var").reshape(2, 4, n_tok * rows, local)
    total_rows = 2 * n_tok * rows

    var_kept = kept[0]
    block = var_kept.shape[0] // n_wide
    names = []
    drops = []
    for i in range(2):
        pair = (row // 2 * 2 + i) * (SIDE // 2) + col // 2
        name = lax.dynamic_slice_in_dim(var_kept, pair * 2 * block, 2 * block) - pair * 2 * local
        names.append(name)
        matches = jnp.arange(2 * local, dtype=jnp.int32)[:, None] == name[None, :]
        drops.append(jnp.where(jnp.any(matches, axis=1), 0.0, 1.0).astype(jnp.bfloat16))
    names = jnp.stack(names)[:, :, None]
    drop = jnp.concatenate(drops).reshape(4, 1, local)

    n_blocks = n_wide // 4
    product_flops = 2 * total_rows * 4 * local * quarter
    shares = call(
        residual_kernel,
        jax.ShapeDtypeStruct((2, total_rows // 2, quarter), jnp.bfloat16),
        [SMEM] + [VMEM] * 6,
        product_flops,
        4 * total_rows * quarter,
    )(slot.reshape(1), hidden, drop, *downs)
    shares = shares.reshape(n_blocks, total_rows // n_blocks, quarter)
    strides = stride_groups()
    shares = lax.all_to_all(shares, "wide", 0, 0, axis_index_groups=strides)
    piece = jnp.sum(shares.astype(jnp.float32), axis=0).astype(jnp.bfloat16)
    rounded = spread(piece, n_blocks, "wide", strides).reshape(total_rows, quarter)

    chosen = call(
        select_kernel,
        jax.ShapeDtypeStruct((2, 2 * block, total_rows), jnp.bfloat16),
        [VMEM] * 2,
        4 * total_rows * local * 4 * block,
        4 * total_rows * local,
    )(names, hidden)
    factor = 1.0 / math.sqrt(total_rows)
    grad, errors = call(
        functools.partial(gradient_kernel, factor),
        (
            jax.ShapeDtypeStruct((4, block, quarter), jnp.bfloat16),
            jax.ShapeDtypeStruct((1, 128), jnp.float32),
        ),
        [VMEM] * 2,
        2 * total_rows * 4 * block * quarter,
        4 * total_rows * quarter,
    )(chosen, rounded)

    for axis, count, flip in (("tok", n_tok, 1), ("tok", n_tok, 2), ("wide", n_wide, 1), ("wide", n_wide, SIDE)):
        errors = errors + lax.ppermute(errors, axis, [(i, i ^ flip) for i in range(count)])
    loss = jnp.sum(errors) / (total_rows * D)

    swapped = lax.all_to_all(grad, "wide", 0, 0, axis_index_groups=blocks)
    grad = call(
        interleave_kernel,
        jax.ShapeDtypeStruct((block, 4 * quarter), jnp.bfloat16),
        [VMEM],
        0,
        4 * block * quarter,
    )(swapped)
    return (loss.reshape(1), grad[None])


def solution(mesh):
    in_specs = (
        P("wide", "tok"),
        P("tok"),
        P("tok", "wide"),
        P("tok", "wide"),
        P("wide", "tok"),
        P("var", None),
    )
    out_specs = (P("var"), P("var", "wide", "tok"))
    return jax.shard_map(
        per_device, mesh=mesh, in_specs=in_specs, out_specs=out_specs, check_vma=False
    )
```

```python
import functools
import math

import jax
import jax.numpy as jnp
from jax import lax
from jax.experimental import pallas as pl
from jax.experimental.pallas import tpu as pltpu
from jax.sharding import PartitionSpec as P

D = 8192
SIDE = 8


def block_groups():
    return [
        [(2 * a + i) * SIDE + 2 * b + j for i in range(2) for j in range(2)]
        for a in range(SIDE // 2)
        for b in range(SIDE // 2)
    ]


def stride_groups():
    return [
        [(2 * a + i) * SIDE + 2 * b + j for a in range(SIDE // 2) for b in range(SIDE // 2)]
        for i in range(2)
        for j in range(2)
    ]


def spread(shard, count, axes, groups=None):
    stacked = jnp.broadcast_to(shard[None], (count,) + shard.shape)
    return lax.all_to_all(stacked, axes, 0, 0, axis_index_groups=groups)


VMEM = pl.BlockSpec(memory_space=pltpu.VMEM)
SMEM = pl.BlockSpec(memory_space=pltpu.SMEM)


def call(kernel, out_shape, in_specs, flops, size):
    out_specs = jax.tree.map(lambda _: VMEM, out_shape)
    return pl.pallas_call(
        kernel,
        out_shape=out_shape,
        in_specs=in_specs,
        out_specs=out_specs,
        compiler_params=pltpu.CompilerParams(vmem_limit_bytes=32 * 1024 * 1024),
        cost_estimate=pl.CostEstimate(flops=flops, bytes_accessed=size, transcendentals=0),
    )


def residual_kernel(slot_ref, own_ref, other_ref, drop_ref, down0, down1, down2, down3, out_ref):
    slot = slot_ref[0]
    downs = (down0, down1, down2, down3)
    for half, hidden_ref in enumerate((own_ref, other_ref)):
        total = None
        for k in range(4):
            index = slot ^ k
            units = hidden_ref[index] * drop_ref[index]
            term = jnp.dot(units, downs[k][...], preferred_element_type=jnp.float32)
            total = term if total is None else total + term
        out_ref[half] = (-total).astype(out_ref.dtype)


def select_kernel(names_ref, own_ref, other_ref, out_ref):
    rows, local = own_ref.shape[1:]
    count = names_ref.shape[1]
    for pair in range(2):
        names = names_ref[pair]
        for half, hidden_ref in enumerate((own_ref, other_ref)):
            total = None
            for i in range(2):
                units = lax.broadcasted_iota(jnp.int32, (count, local), 1) + i * local
                picker = jnp.where(units == names, 1.0, 0.0).astype(jnp.bfloat16)
                term = lax.dot_general(
                    picker,
                    hidden_ref[2 * pair + i],
                    (((1,), (1,)), ((), ())),
                    preferred_element_type=jnp.float32,
                )
                total = term if total is None else total + term
            out_ref[pair, :, half * rows : (half + 1) * rows] = total.astype(out_ref.dtype)


def gradient_kernel(factor, chosen_ref, rounded_ref, grad_ref, error_ref):
    rounded = rounded_ref[...]
    block = grad_ref.shape[1]
    for pair in range(2):
        product = jnp.dot(chosen_ref[pair], rounded, preferred_element_type=jnp.float32) * factor
        for i in range(2):
            grad_ref[2 * pair + i] = product[i * block : (i + 1) * block].astype(grad_ref.dtype)
    errors = rounded.astype(jnp.float32)
    columns = jnp.sum(errors * errors, axis=0, keepdims=True)
    total = columns[:, :128]
    for i in range(1, columns.shape[1] // 128):
        total = total + columns[:, i * 128 : (i + 1) * 128]
    error_ref[...] = total


def interleave_kernel(in_ref, out_ref):
    width = in_ref.shape[2]
    for i in range(in_ref.shape[0]):
        out_ref[:, i * width : (i + 1) * width] = in_ref[i]


def per_device(tokens, norm_gain, gate_parent, up_parent, down_parent, kept):
    n_wide = lax.axis_size("wide")
    n_tok = lax.axis_size("tok")
    core = lax.axis_index("var")
    wide = lax.axis_index("wide")
    row, col = wide // SIDE, wide % SIDE
    slot = (row % 2) * 2 + col % 2
    local = gate_parent.shape[1]
    width = tokens.shape[1]
    blocks = block_groups()

    half = tokens.shape[0] // 2
    mine = lax.dynamic_slice_in_dim(tokens, core * half, half, 0)
    gathered = spread(mine, n_wide, "wide").reshape(n_wide * half, width)

    widths = gathered.astype(jnp.float32)
    squares = jnp.sum(widths * widths, axis=1)
    gained = (widths * norm_gain[None, :]).astype(jnp.bfloat16)
    partial = jnp.concatenate(
        [
            jnp.dot(gained, gate_parent, preferred_element_type=jnp.float32),
            jnp.dot(gained, up_parent, preferred_element_type=jnp.float32),
            jnp.broadcast_to(squares[:, None], (n_wide * half, 128)),
        ],
        axis=1,
    )
    rows = n_wide * half // n_tok

    quarter = down_parent.shape[1] // 4
    partial, down = lax.optimization_barrier((partial, down_parent))
    downs = [lax.dynamic_slice_in_dim(down, (slot ^ k) * quarter, quarter, 1) for k in range(4)]
    for k in range(1, 4):
        perm = [(w, w ^ ((k // 2) * SIDE + k % 2)) for w in range(n_wide)]
        downs[k] = lax.ppermute(downs[k], "wide", perm)

    scattered = lax.all_to_all(partial.reshape(n_tok, rows, 2 * local + 128), "tok", 0, 0)
    scattered, *downs = lax.optimization_barrier((scattered, *downs))
    total = jnp.sum(scattered, axis=0)
    scale = lax.rsqrt(total[:, 2 * local :][:, :1] / D + 1e-05)
    gate = total[:, :local] * scale
    up = total[:, local : 2 * local] * scale
    hidden = (jax.nn.silu(gate) * up).astype(jnp.bfloat16)

    groups = [[t * n_wide + w for w in block for t in range(n_tok)] for block in blocks]
    hidden = spread(hidden, n_tok * 4, ("tok", "wide"), groups)
    hidden = hidden.reshape(4, n_tok * rows, local)
    other = lax.ppermute(hidden, "var", [(0, 1), (1, 0)])
    total_rows = 2 * n_tok * rows

    var_kept = kept[0]
    block = var_kept.shape[0] // n_wide
    names = []
    drops = []
    for i in range(2):
        pair = (row // 2 * 2 + i) * (SIDE // 2) + col // 2
        name = lax.dynamic_slice_in_dim(var_kept, pair * 2 * block, 2 * block) - pair * 2 * local
        names.append(name)
        matches = jnp.arange(2 * local, dtype=jnp.int32)[:, None] == name[None, :]
        drops.append(jnp.where(jnp.any(matches, axis=1), 0.0, 1.0).astype(jnp.bfloat16))
    names = jnp.stack(names)[:, :, None]
    drop = jnp.concatenate(drops).reshape(4, 1, local)

    n_blocks = n_wide // 4
    product_flops = 2 * total_rows * 4 * local * quarter
    shares = call(
        residual_kernel,
        jax.ShapeDtypeStruct((2, total_rows // 2, quarter), jnp.bfloat16),
        [SMEM] + [VMEM] * 7,
        product_flops,
        4 * total_rows * quarter,
    )(slot.reshape(1), hidden, other, drop, *downs)
    shares = shares.reshape(n_blocks, total_rows // n_blocks, quarter)
    strides = stride_groups()
    shares = lax.all_to_all(shares, "wide", 0, 0, axis_index_groups=strides)
    piece = jnp.sum(shares.astype(jnp.float32), axis=0).astype(jnp.bfloat16)
    rounded = spread(piece, n_blocks, "wide", strides).reshape(total_rows, quarter)

    chosen = call(
        select_kernel,
        jax.ShapeDtypeStruct((2, 2 * block, total_rows), jnp.bfloat16),
        [VMEM] * 3,
        4 * total_rows * local * 4 * block,
        4 * total_rows * local,
    )(names, hidden, other)
    factor = 1.0 / math.sqrt(total_rows)
    grad, errors = call(
        functools.partial(gradient_kernel, factor),
        (
            jax.ShapeDtypeStruct((4, block, quarter), jnp.bfloat16),
            jax.ShapeDtypeStruct((1, 128), jnp.float32),
        ),
        [VMEM] * 2,
        2 * total_rows * 4 * block * quarter,
        4 * total_rows * quarter,
    )(chosen, rounded)

    errors = lax.psum(lax.psum(errors, "tok"), "wide", axis_index_groups=blocks)
    loss = jnp.sum(errors) / (total_rows * D)

    swapped = lax.all_to_all(grad, "wide", 0, 0, axis_index_groups=blocks)
    grad = call(
        interleave_kernel,
        jax.ShapeDtypeStruct((block, 4 * quarter), jnp.bfloat16),
        [VMEM],
        0,
        4 * block * quarter,
    )(swapped)
    return (loss.reshape(1), grad[None])


def solution(mesh):
    in_specs = (
        P("wide", "tok"),
        P("tok"),
        P("tok", "wide"),
        P("tok", "wide"),
        P("wide", "tok"),
        P("var", None),
    )
    out_specs = (P("var"), P("var", "wide", "tok"))
    return jax.shard_map(
        per_device, mesh=mesh, in_specs=in_specs, out_specs=out_specs, check_vma=False
    )
```

```python
import functools
import math

import jax
import jax.numpy as jnp
from jax import lax
from jax.experimental import pallas as pl
from jax.experimental.pallas import tpu as pltpu
from jax.sharding import PartitionSpec as P

D = 8192
SIDE = 8


def block_groups():
    return [
        [(2 * a + i) * SIDE + 2 * b + j for i in range(2) for j in range(2)]
        for a in range(SIDE // 2)
        for b in range(SIDE // 2)
    ]


def stride_groups():
    return [
        [(2 * a + i) * SIDE + 2 * b + j for a in range(SIDE // 2) for b in range(SIDE // 2)]
        for i in range(2)
        for j in range(2)
    ]


def spread(shard, count, axes, groups=None):
    stacked = jnp.broadcast_to(shard[None], (count,) + shard.shape)
    return lax.all_to_all(stacked, axes, 0, 0, axis_index_groups=groups)


def hi_lo(value):
    hi = lax.reduce_precision(value, 8, 7)
    return hi.astype(jnp.bfloat16), (value - hi).astype(jnp.bfloat16)


VMEM = pl.BlockSpec(memory_space=pltpu.VMEM)
SMEM = pl.BlockSpec(memory_space=pltpu.SMEM)


def call(kernel, out_shape, in_specs, flops, size):
    out_specs = jax.tree.map(lambda _: VMEM, out_shape)
    return pl.pallas_call(
        kernel,
        out_shape=out_shape,
        in_specs=in_specs,
        out_specs=out_specs,
        compiler_params=pltpu.CompilerParams(vmem_limit_bytes=32 * 1024 * 1024),
        cost_estimate=pl.CostEstimate(flops=flops, bytes_accessed=size, transcendentals=0),
    )


def residual_kernel(slot_ref, hidden_ref, drop_ref, down0, down1, down2, down3, out_ref):
    slot = slot_ref[0]
    downs = (down0, down1, down2, down3)
    for core in range(2):
        total = None
        for k in range(4):
            index = slot ^ k
            units = hidden_ref[core, index] * drop_ref[index]
            term = jnp.dot(units, downs[k][...], preferred_element_type=jnp.float32)
            total = term if total is None else total + term
        out_ref[core] = (-total).astype(out_ref.dtype)


def select_kernel(names_ref, hidden_ref, out_ref):
    local = hidden_ref.shape[3]
    rows = hidden_ref.shape[2]
    count = names_ref.shape[1]
    for pair in range(2):
        names = names_ref[pair]
        for core in range(2):
            total = None
            for i in range(2):
                units = lax.broadcasted_iota(jnp.int32, (count, local), 1) + i * local
                picker = jnp.where(units == names, 1.0, 0.0).astype(jnp.bfloat16)
                term = lax.dot_general(
                    picker,
                    hidden_ref[core, 2 * pair + i],
                    (((1,), (1,)), ((), ())),
                    preferred_element_type=jnp.float32,
                )
                total = term if total is None else total + term
            out_ref[pair, :, core * rows : (core + 1) * rows] = total.astype(out_ref.dtype)


def gradient_kernel(factor, chosen_ref, rounded_ref, grad_ref, error_ref):
    rounded = rounded_ref[...]
    block = grad_ref.shape[1]
    for pair in range(2):
        product = jnp.dot(chosen_ref[pair], rounded, preferred_element_type=jnp.float32) * factor
        for i in range(2):
            grad_ref[2 * pair + i] = product[i * block : (i + 1) * block].astype(grad_ref.dtype)
    errors = rounded.astype(jnp.float32)
    columns = jnp.sum(errors * errors, axis=0, keepdims=True)
    total = columns[:, :128]
    for i in range(1, columns.shape[1] // 128):
        total = total + columns[:, i * 128 : (i + 1) * 128]
    error_ref[...] = total


def interleave_kernel(in_ref, out_ref):
    width = in_ref.shape[2]
    for i in range(in_ref.shape[0]):
        out_ref[:, i * width : (i + 1) * width] = in_ref[i]


def per_device(tokens, norm_gain, gate_parent, up_parent, down_parent, kept):
    n_wide = lax.axis_size("wide")
    n_tok = lax.axis_size("tok")
    core = lax.axis_index("var")
    wide = lax.axis_index("wide")
    row, col = wide // SIDE, wide % SIDE
    slot = (row % 2) * 2 + col % 2
    local = gate_parent.shape[1]
    width = tokens.shape[1]
    blocks = block_groups()

    half = tokens.shape[0] // 2
    mine = lax.dynamic_slice_in_dim(tokens, core * half, half, 0)
    gathered = spread(mine, n_wide, "wide").reshape(n_wide * half, width)

    quarter = down_parent.shape[1] // 4
    downs = [lax.dynamic_slice_in_dim(down_parent, (slot ^ k) * quarter, quarter, 1) for k in range(4)]
    for k in range(1, 4):
        perm = [(w, w ^ ((k // 2) * SIDE + k % 2)) for w in range(n_wide)]
        downs[k] = lax.ppermute(downs[k], "wide", perm)
    gathered, *downs = lax.optimization_barrier((gathered, *downs))

    widths = gathered.astype(jnp.float32)
    squares = jnp.sum(widths * widths, axis=1)
    gained = (widths * norm_gain[None, :]).astype(jnp.bfloat16)
    sq_hi, sq_lo = hi_lo(squares)
    lanes = lax.broadcasted_iota(jnp.int32, (n_wide * half, 128), 1)
    extra = jnp.where(lanes == 0, sq_hi[:, None], jnp.where(lanes == 1, sq_lo[:, None], jnp.zeros((), jnp.bfloat16)))
    partial = jnp.concatenate(
        [
            jnp.dot(gained, gate_parent, preferred_element_type=jnp.float32).astype(jnp.bfloat16),
            jnp.dot(gained, up_parent, preferred_element_type=jnp.float32).astype(jnp.bfloat16),
            extra,
        ],
        axis=1,
    )
    rows = n_wide * half // n_tok

    scattered = lax.all_to_all(partial.reshape(n_tok, rows, 2 * local + 128), "tok", 0, 0)
    total = jnp.sum(scattered.astype(jnp.float32), axis=0)
    scale = lax.rsqrt((total[:, 2 * local] + total[:, 2 * local + 1]) / D + 1e-05)[:, None]
    gate = total[:, :local] * scale
    up = total[:, local : 2 * local] * scale
    hidden = (jax.nn.silu(gate) * up).astype(jnp.bfloat16)

    groups = [[t * n_wide + w for w in block for t in range(n_tok)] for block in blocks]
    hidden = spread(hidden, n_tok * 4, ("tok", "wide"), groups)
    hidden = spread(hidden, 2, "var").reshape(2, 4, n_tok * rows, local)
    total_rows = 2 * n_tok * rows

    var_kept = kept[0]
    block = var_kept.shape[0] // n_wide
    names = []
    drops = []
    for i in range(2):
        pair = (row // 2 * 2 + i) * (SIDE // 2) + col // 2
        name = lax.dynamic_slice_in_dim(var_kept, pair * 2 * block, 2 * block) - pair * 2 * local
        names.append(name)
        matches = jnp.arange(2 * local, dtype=jnp.int32)[:, None] == name[None, :]
        drops.append(jnp.where(jnp.any(matches, axis=1), 0.0, 1.0).astype(jnp.bfloat16))
    names = jnp.stack(names)[:, :, None]
    drop = jnp.concatenate(drops).reshape(4, 1, local)

    n_blocks = n_wide // 4
    product_flops = 2 * total_rows * 4 * local * quarter
    shares = call(
        residual_kernel,
        jax.ShapeDtypeStruct((2, total_rows // 2, quarter), jnp.bfloat16),
        [SMEM] + [VMEM] * 6,
        product_flops,
        4 * total_rows * quarter,
    )(slot.reshape(1), hidden, drop, *downs)
    shares = shares.reshape(n_blocks, total_rows // n_blocks, quarter)
    strides = stride_groups()
    shares = lax.all_to_all(shares, "wide", 0, 0, axis_index_groups=strides)
    piece = jnp.sum(shares.astype(jnp.float32), axis=0).astype(jnp.bfloat16)
    rounded = spread(piece, n_blocks, "wide", strides).reshape(total_rows, quarter)

    chosen = call(
        select_kernel,
        jax.ShapeDtypeStruct((2, 2 * block, total_rows), jnp.bfloat16),
        [VMEM] * 2,
        4 * total_rows * local * 4 * block,
        4 * total_rows * local,
    )(names, hidden)
    factor = 1.0 / math.sqrt(total_rows)
    grad, errors = call(
        functools.partial(gradient_kernel, factor),
        (
            jax.ShapeDtypeStruct((4, block, quarter), jnp.bfloat16),
            jax.ShapeDtypeStruct((1, 128), jnp.float32),
        ),
        [VMEM] * 2,
        2 * total_rows * 4 * block * quarter,
        4 * total_rows * quarter,
    )(chosen, rounded)

    errors = lax.psum(lax.psum(errors, "tok"), "wide", axis_index_groups=blocks)
    loss = jnp.sum(errors) / (total_rows * D)

    swapped = lax.all_to_all(grad, "wide", 0, 0, axis_index_groups=blocks)
    grad = call(
        interleave_kernel,
        jax.ShapeDtypeStruct((block, 4 * quarter), jnp.bfloat16),
        [VMEM],
        0,
        4 * block * quarter,
    )(swapped)
    return (loss.reshape(1), grad[None])


def solution(mesh):
    in_specs = (
        P("wide", "tok"),
        P("tok"),
        P("tok", "wide"),
        P("tok", "wide"),
        P("wide", "tok"),
        P("var", None),
    )
    out_specs = (P("var"), P("var", "wide", "tok"))
    return jax.shard_map(
        per_device, mesh=mesh, in_specs=in_specs, out_specs=out_specs, check_vma=False
    )
```

```python
import functools
import math

import jax
import jax.numpy as jnp
from jax import lax
from jax.experimental import pallas as pl
from jax.experimental.pallas import tpu as pltpu
from jax.sharding import PartitionSpec as P

D = 8192
SIDE = 8


def block_groups():
    return [
        [(2 * a + i) * SIDE + 2 * b + j for i in range(2) for j in range(2)]
        for a in range(SIDE // 2)
        for b in range(SIDE // 2)
    ]


def stride_groups():
    return [
        [(2 * a + i) * SIDE + 2 * b + j for a in range(SIDE // 2) for b in range(SIDE // 2)]
        for i in range(2)
        for j in range(2)
    ]


def spread(shard, count, axes, groups=None):
    stacked = jnp.broadcast_to(shard[None], (count,) + shard.shape)
    return lax.all_to_all(stacked, axes, 0, 0, axis_index_groups=groups)


def hi_lo(value):
    hi = lax.reduce_precision(value, 8, 7)
    return hi.astype(jnp.bfloat16), (value - hi).astype(jnp.bfloat16)


VMEM = pl.BlockSpec(memory_space=pltpu.VMEM)
SMEM = pl.BlockSpec(memory_space=pltpu.SMEM)


def call(kernel, out_shape, in_specs, flops, size):
    out_specs = jax.tree.map(lambda _: VMEM, out_shape)
    return pl.pallas_call(
        kernel,
        out_shape=out_shape,
        in_specs=in_specs,
        out_specs=out_specs,
        compiler_params=pltpu.CompilerParams(vmem_limit_bytes=16 * 1024 * 1024),
        cost_estimate=pl.CostEstimate(flops=flops, bytes_accessed=size, transcendentals=0),
    )


def residual_kernel(slot_ref, hidden_ref, drop_ref, down0, down1, down2, down3, out_ref):
    slot = slot_ref[0]
    downs = (down0, down1, down2, down3)
    for core in range(2):
        total = None
        for k in range(4):
            index = slot ^ k
            units = hidden_ref[core, index] * drop_ref[index]
            term = jnp.dot(units, downs[k][...], preferred_element_type=jnp.float32)
            total = term if total is None else total + term
        out_ref[core] = (-total).astype(out_ref.dtype)


def select_kernel(names_ref, hidden_ref, out_ref):
    local = hidden_ref.shape[3]
    rows = hidden_ref.shape[2]
    count = names_ref.shape[1]
    for pair in range(2):
        names = names_ref[pair]
        for core in range(2):
            total = None
            for i in range(2):
                units = lax.broadcasted_iota(jnp.int32, (count, local), 1) + i * local
                picker = jnp.where(units == names, 1.0, 0.0).astype(jnp.bfloat16)
                term = lax.dot_general(
                    picker,
                    hidden_ref[core, 2 * pair + i],
                    (((1,), (1,)), ((), ())),
                    preferred_element_type=jnp.float32,
                )
                total = term if total is None else total + term
            out_ref[pair, :, core * rows : (core + 1) * rows] = total.astype(out_ref.dtype)


def hidden_kernel(sums_ref, out_ref):
    local = out_ref.shape[2]
    total = sums_ref[0].astype(jnp.float32)
    for i in range(1, sums_ref.shape[0]):
        total = total + sums_ref[i].astype(jnp.float32)
    squares = total[:, local : local + 1] + total[:, local + 1 : local + 2]
    scale = lax.rsqrt(squares / D + 1e-05)
    half = total.shape[1] // 2
    gate = total[:, :local] * scale
    up = total[:, half : half + local] * scale
    hidden = (gate / (1.0 + jnp.exp(-gate)) * up).astype(out_ref.dtype)
    for i in range(out_ref.shape[0]):
        out_ref[i] = hidden


def piece_kernel(shares_ref, out_ref):
    total = shares_ref[0].astype(jnp.float32)
    for i in range(1, shares_ref.shape[0]):
        total = total + shares_ref[i].astype(jnp.float32)
    piece = total.astype(out_ref.dtype)
    for i in range(out_ref.shape[0]):
        out_ref[i] = piece


def gradient_kernel(factor, chosen_ref, rounded_ref, out_ref):
    rounded = rounded_ref[...]
    block = chosen_ref.shape[1] // 2
    for pair in range(2):
        product = jnp.dot(chosen_ref[pair], rounded, preferred_element_type=jnp.float32) * factor
        for i in range(2):
            out_ref[2 * pair + i, :block] = product[i * block : (i + 1) * block].astype(out_ref.dtype)
    errors = rounded.astype(jnp.float32)
    columns = jnp.sum(errors * errors, axis=0, keepdims=True)
    hi = columns.astype(out_ref.dtype).astype(jnp.float32)
    line = lax.broadcasted_iota(jnp.int32, (16, columns.shape[1]), 0)
    extra = jnp.where(line == 0, hi, jnp.where(line == 1, columns - hi, 0.0)).astype(out_ref.dtype)
    for i in range(4):
        out_ref[i, block:] = extra


def interleave_kernel(in_ref, out_ref, error_ref):
    block = out_ref.shape[0]
    width = in_ref.shape[2]
    total = None
    for i in range(in_ref.shape[0]):
        out_ref[:, i * width : (i + 1) * width] = in_ref[i, :block]
        term = in_ref[i, block:].astype(jnp.float32)
        total = term if total is None else total + term
    columns = jnp.sum(total, axis=0, keepdims=True)
    lanes = columns[:, :128]
    for i in range(1, width // 128):
        lanes = lanes + columns[:, i * 128 : (i + 1) * 128]
    error_ref[...] = lanes


def per_device(tokens, norm_gain, gate_parent, up_parent, down_parent, kept):
    n_wide = lax.axis_size("wide")
    n_tok = lax.axis_size("tok")
    core = lax.axis_index("var")
    wide = lax.axis_index("wide")
    row, col = wide // SIDE, wide % SIDE
    slot = (row % 2) * 2 + col % 2
    local = gate_parent.shape[1]
    width = tokens.shape[1]
    blocks = block_groups()

    half = tokens.shape[0] // 2
    mine = lax.dynamic_slice_in_dim(tokens, core * half, half, 0)
    gathered = spread(mine, n_wide, "wide").reshape(n_wide * half, width)

    quarter = down_parent.shape[1] // 4
    downs = [lax.dynamic_slice_in_dim(down_parent, (slot ^ k) * quarter, quarter, 1) for k in range(4)]
    for k in range(1, 4):
        perm = [(w, w ^ ((k // 2) * SIDE + k % 2)) for w in range(n_wide)]
        downs[k] = lax.ppermute(downs[k], "wide", perm)

    widths = gathered.astype(jnp.float32)
    squares = jnp.sum(widths * widths, axis=1)
    gained = (widths * norm_gain[None, :]).astype(jnp.bfloat16)
    sq_hi, sq_lo = hi_lo(squares)
    pad = (-local) % 128
    lanes = lax.broadcasted_iota(jnp.int32, (n_wide * half, pad), 1)
    extra = jnp.where(lanes == 0, sq_hi[:, None], jnp.where(lanes == 1, sq_lo[:, None], jnp.zeros((), jnp.bfloat16)))
    partial = jnp.concatenate(
        [
            jnp.dot(gained, gate_parent, preferred_element_type=jnp.float32).astype(jnp.bfloat16),
            extra,
            jnp.dot(gained, up_parent, preferred_element_type=jnp.float32).astype(jnp.bfloat16),
            jnp.zeros((n_wide * half, pad), jnp.bfloat16),
        ],
        axis=1,
    )
    rows = n_wide * half // n_tok

    scattered = lax.all_to_all(partial.reshape(n_tok, rows, 2 * (local + pad)), "tok", 0, 0)
    scattered, *downs = lax.optimization_barrier((scattered, *downs))
    hidden = call(
        hidden_kernel,
        jax.ShapeDtypeStruct((4 * n_tok, rows, local), jnp.bfloat16),
        [VMEM],
        0,
        16 * rows * local,
    )(scattered)

    groups = [[t * n_wide + w for w in block for t in range(n_tok)] for block in blocks]
    hidden = lax.all_to_all(hidden, ("tok", "wide"), 0, 0, axis_index_groups=groups)
    hidden = spread(hidden, 2, "var").reshape(2, 4, n_tok * rows, local)
    total_rows = 2 * n_tok * rows

    var_kept = kept[0]
    block = var_kept.shape[0] // n_wide
    names = []
    drops = []
    for i in range(2):
        pair = (row // 2 * 2 + i) * (SIDE // 2) + col // 2
        name = lax.dynamic_slice_in_dim(var_kept, pair * 2 * block, 2 * block) - pair * 2 * local
        names.append(name)
        matches = jnp.arange(2 * local, dtype=jnp.int32)[:, None] == name[None, :]
        drops.append(jnp.where(jnp.any(matches, axis=1), 0.0, 1.0).astype(jnp.bfloat16))
    names = jnp.stack(names)[:, :, None]
    drop = jnp.concatenate(drops).reshape(4, 1, local)

    n_blocks = n_wide // 4
    product_flops = 2 * total_rows * 4 * local * quarter
    shares = call(
        residual_kernel,
        jax.ShapeDtypeStruct((2, total_rows // 2, quarter), jnp.bfloat16),
        [SMEM] + [VMEM] * 6,
        product_flops,
        4 * total_rows * quarter,
    )(slot.reshape(1), hidden, drop, *downs)
    shares = shares.reshape(n_blocks, total_rows // n_blocks, quarter)
    strides = stride_groups()
    shares = lax.all_to_all(shares, "wide", 0, 0, axis_index_groups=strides)
    pieces = call(piece_kernel, jax.ShapeDtypeStruct(shares.shape, jnp.bfloat16), [VMEM], 0, 4 * total_rows * quarter)(shares)
    rounded = lax.all_to_all(pieces, "wide", 0, 0, axis_index_groups=strides).reshape(total_rows, quarter)

    chosen = call(
        select_kernel,
        jax.ShapeDtypeStruct((2, 2 * block, total_rows), jnp.bfloat16),
        [VMEM] * 2,
        4 * total_rows * local * 4 * block,
        4 * total_rows * local,
    )(names, hidden)
    factor = 1.0 / math.sqrt(total_rows)
    grad = call(
        functools.partial(gradient_kernel, factor),
        jax.ShapeDtypeStruct((4, block + 16, quarter), jnp.bfloat16),
        [VMEM] * 2,
        2 * total_rows * 4 * block * quarter,
        4 * total_rows * quarter,
    )(chosen, rounded)
    swapped = lax.all_to_all(grad, "wide", 0, 0, axis_index_groups=blocks)
    grad, errors = call(
        interleave_kernel,
        (
            jax.ShapeDtypeStruct((block, 4 * quarter), jnp.bfloat16),
            jax.ShapeDtypeStruct((1, 128), jnp.float32),
        ),
        [VMEM],
        0,
        4 * block * quarter,
    )(swapped)
    loss = jnp.sum(lax.psum(errors, "tok")) / (total_rows * D)
    return (loss.reshape(1), grad[None])


def solution(mesh):
    in_specs = (
        P("wide", "tok"),
        P("tok"),
        P("tok", "wide"),
        P("tok", "wide"),
        P("wide", "tok"),
        P("var", None),
    )
    out_specs = (P("var"), P("var", "wide", "tok"))
    return jax.shard_map(
        per_device, mesh=mesh, in_specs=in_specs, out_specs=out_specs, check_vma=False
    )
```

```python
import functools
import math

import jax
import jax.numpy as jnp
from jax import lax
from jax.experimental import pallas as pl
from jax.experimental.pallas import tpu as pltpu
from jax.sharding import PartitionSpec as P

D = 8192
SIDE = 8


def block_groups():
    return [
        [(2 * a + i) * SIDE + 2 * b + j for i in range(2) for j in range(2)]
        for a in range(SIDE // 2)
        for b in range(SIDE // 2)
    ]


def stride_groups():
    return [
        [(2 * a + i) * SIDE + 2 * b + j for a in range(SIDE // 2) for b in range(SIDE // 2)]
        for i in range(2)
        for j in range(2)
    ]


VMEM = pl.BlockSpec(memory_space=pltpu.VMEM)
SMEM = pl.BlockSpec(memory_space=pltpu.SMEM)


def call(kernel, out_shape, in_specs, flops, size, scratch=()):
    out_specs = jax.tree.map(lambda _: VMEM, out_shape)
    return pl.pallas_call(
        kernel,
        out_shape=out_shape,
        in_specs=in_specs,
        out_specs=out_specs,
        scratch_shapes=list(scratch),
        compiler_params=pltpu.CompilerParams(vmem_limit_bytes=16 * 1024 * 1024),
        cost_estimate=pl.CostEstimate(flops=flops, bytes_accessed=size, transcendentals=0),
    )


def spread_kernel(place_ref, tokens_ref, out_ref):
    width = out_ref.shape[2]
    tokens = tokens_ref[...].astype(jnp.float32)
    left, right = tokens[:, :width], tokens[:, width:]
    odd = place_ref[1] == 1
    first = jnp.where(odd, right, left)
    second = jnp.where(odd, left, right)
    upper = lax.broadcasted_iota(jnp.int32, first.shape, 0) < 4
    low = jnp.where(upper, first, pltpu.roll(second, 4, 0))
    high = jnp.where(upper, pltpu.roll(first, 4, 0), second)
    piece = jnp.where(place_ref[0] == 0, low, high).astype(out_ref.dtype)
    for i in range(out_ref.shape[0]):
        out_ref[i] = piece


def parent_kernel(tokens_ref, gain_ref, gate_ref, up_ref, out_ref, rows_ref):
    n_shards, _, width = tokens_ref.shape
    local = gate_ref.shape[0]
    lanes = out_ref.shape[1] // 2
    step = 16
    squares = []
    for i in range(0, n_shards, step):
        part = tokens_ref[i : i + step].astype(jnp.float32).reshape(step // 2, 2, 8, width)
        even, odd = part[:, 0], part[:, 1]
        upper = lax.broadcasted_iota(jnp.int32, even.shape, 1) < 4
        left = jnp.where(upper, even, odd)
        right = jnp.where(upper, odd, even)
        rows = slice(i * 4, (i + step) * 4)
        left = left.reshape(step * 4, width)
        right = pltpu.roll(right, 4, 1).reshape(step * 4, width)
        squares.append(jnp.sum(left * left + right * right, axis=1, keepdims=True))
        rows_ref[rows, :width] = (left * gain_ref[:, :width]).astype(rows_ref.dtype)
        rows_ref[rows, width:] = (right * gain_ref[:, width:]).astype(rows_ref.dtype)
    squares = jnp.concatenate(squares, axis=0)
    hi = squares.astype(jnp.bfloat16).astype(jnp.float32)
    contract = (((1,), (1,)), ((), ()))
    gate = lax.dot_general(rows_ref[...], gate_ref[...], contract, preferred_element_type=jnp.float32)
    up = lax.dot_general(rows_ref[...], up_ref[...], contract, preferred_element_type=jnp.float32)
    lane = lax.broadcasted_iota(jnp.int32, (squares.shape[0], lanes - local), 1)
    extra = jnp.where(lane == 0, hi, jnp.where(lane == 1, squares - hi, 0.0))
    out_ref[:, :local] = gate.astype(out_ref.dtype)
    out_ref[:, local:lanes] = extra.astype(out_ref.dtype)
    out_ref[:, lanes : lanes + local] = up.astype(out_ref.dtype)
    out_ref[:, lanes + local :] = jnp.zeros_like(extra).astype(out_ref.dtype)


def residual_kernel(slot_ref, own_ref, other_ref, drop_ref, down0, down1, down2, down3, out_ref):
    slot = slot_ref[0]
    downs = (down0, down1, down2, down3)
    local = down0.shape[0]
    for half, hidden_ref in enumerate((own_ref, other_ref)):
        total = None
        for k in range(4):
            index = slot ^ k
            units = hidden_ref[index][:, :local] * drop_ref[index]
            term = jnp.dot(units, downs[k][...], preferred_element_type=jnp.float32)
            total = term if total is None else total + term
        out_ref[half] = (-total).astype(out_ref.dtype)


def select_kernel(names_ref, own_ref, other_ref, out_ref):
    rows = own_ref.shape[1]
    count = names_ref.shape[1]
    local = count
    for pair in range(2):
        names = names_ref[pair]
        for half, hidden_ref in enumerate((own_ref, other_ref)):
            total = None
            for i in range(2):
                units = lax.broadcasted_iota(jnp.int32, (count, local), 1) + i * local
                picker = jnp.where(units == names, 1.0, 0.0).astype(jnp.bfloat16)
                term = lax.dot_general(
                    picker,
                    hidden_ref[2 * pair + i][:, :local],
                    (((1,), (1,)), ((), ())),
                    preferred_element_type=jnp.float32,
                )
                total = term if total is None else total + term
            out_ref[pair, :, half * rows : (half + 1) * rows] = total.astype(out_ref.dtype)


def hidden_kernel(local, sums_ref, out_ref):
    total = sums_ref[0].astype(jnp.float32)
    for i in range(1, sums_ref.shape[0]):
        total = total + sums_ref[i].astype(jnp.float32)
    squares = total[:, local : local + 1] + total[:, local + 1 : local + 2]
    scale = lax.rsqrt(squares / D + 1e-05)
    half = total.shape[1] // 2
    gate = total[:, :half] * scale
    up = total[:, half:] * scale
    hidden = (gate / (1.0 + jnp.exp(-gate)) * up).astype(out_ref.dtype)
    for i in range(out_ref.shape[0]):
        out_ref[i] = hidden


def piece_kernel(shares_ref, out_ref):
    total = shares_ref[0].astype(jnp.float32)
    for i in range(1, shares_ref.shape[0]):
        total = total + shares_ref[i].astype(jnp.float32)
    piece = total.astype(out_ref.dtype)
    for i in range(out_ref.shape[0]):
        out_ref[i] = piece


def gradient_kernel(factor, chosen_ref, rounded_ref, out_ref):
    rounded = rounded_ref[...]
    block = chosen_ref.shape[1] // 2
    for pair in range(2):
        product = jnp.dot(chosen_ref[pair], rounded, preferred_element_type=jnp.float32) * factor
        for i in range(2):
            out_ref[2 * pair + i, :block] = product[i * block : (i + 1) * block].astype(out_ref.dtype)
    errors = rounded.astype(jnp.float32)
    columns = jnp.sum(errors * errors, axis=0, keepdims=True)
    hi = columns.astype(out_ref.dtype).astype(jnp.float32)
    line = lax.broadcasted_iota(jnp.int32, (16, columns.shape[1]), 0)
    extra = jnp.where(line == 0, hi, jnp.where(line == 1, columns - hi, 0.0)).astype(out_ref.dtype)
    for i in range(4):
        out_ref[i, block:] = extra


def interleave_kernel(in_ref, out_ref, error_ref):
    block = out_ref.shape[0]
    width = in_ref.shape[2]
    total = None
    for i in range(in_ref.shape[0]):
        out_ref[:, i * width : (i + 1) * width] = in_ref[i, :block]
        term = in_ref[i, block:].astype(jnp.float32)
        total = term if total is None else total + term
    columns = jnp.sum(total, axis=0, keepdims=True)
    lanes = columns[:, :128]
    for i in range(1, width // 128):
        lanes = lanes + columns[:, i * 128 : (i + 1) * 128]
    line = lax.broadcasted_iota(jnp.int32, (8, 128), 0)
    lanes = jnp.where(line == 0, lanes, 0.0)
    for i in range(error_ref.shape[0]):
        error_ref[i] = lanes


def per_device(tokens, norm_gain, gate_parent, up_parent, down_parent, kept):
    n_wide = lax.axis_size("wide")
    n_tok = lax.axis_size("tok")
    core = lax.axis_index("var")
    wide = lax.axis_index("wide")
    row, col = wide // SIDE, wide % SIDE
    slot = (row % 2) * 2 + col % 2
    local = gate_parent.shape[1]
    width = tokens.shape[1]
    blocks = block_groups()

    half = tokens.shape[0] // 2
    pieces = call(
        spread_kernel,
        jax.ShapeDtypeStruct((n_wide, 2 * half, width // 2), jnp.bfloat16),
        [SMEM, VMEM],
        0,
        2 * n_wide * half * width,
    )(jnp.stack([core, wide % 2]), tokens)
    gathered = lax.all_to_all(pieces, "wide", 0, 0)

    quarter = down_parent.shape[1] // 4
    downs = [lax.dynamic_slice_in_dim(down_parent, (slot ^ k) * quarter, quarter, 1) for k in range(4)]
    for k in range(1, 4):
        perm = [(w, w ^ ((k // 2) * SIDE + k % 2)) for w in range(n_wide)]
        downs[k] = lax.ppermute(downs[k], "wide", perm)

    pad = (-local) % 128
    partial = call(
        parent_kernel,
        jax.ShapeDtypeStruct((n_wide * half, 2 * (local + pad)), jnp.bfloat16),
        [VMEM] * 4,
        4 * n_wide * half * width * local,
        8 * width * local,
        [pltpu.VMEM((n_wide * half, width), jnp.bfloat16)],
    )(gathered, norm_gain.reshape(1, width), gate_parent.T, up_parent.T)
    rows = n_wide * half // n_tok

    scattered = lax.all_to_all(partial.reshape(n_tok, rows, 2 * (local + pad)), "tok", 0, 0)
    scattered, *downs = lax.optimization_barrier((scattered, *downs))
    hidden = call(
        functools.partial(hidden_kernel, local),
        jax.ShapeDtypeStruct((4 * n_tok, rows, local + pad), jnp.bfloat16),
        [VMEM],
        0,
        16 * rows * local,
    )(scattered)

    groups = [[t * n_wide + w for w in block for t in range(n_tok)] for block in blocks]
    hidden = lax.all_to_all(hidden, ("tok", "wide"), 0, 0, axis_index_groups=groups)
    hidden = hidden.reshape(4, n_tok * rows, local + pad)
    other = lax.ppermute(hidden, "var", [(0, 1), (1, 0)])
    total_rows = 2 * n_tok * rows

    var_kept = kept[0]
    block = var_kept.shape[0] // n_wide
    names = []
    drops = []
    for i in range(2):
        pair = (row // 2 * 2 + i) * (SIDE // 2) + col // 2
        name = lax.dynamic_slice_in_dim(var_kept, pair * 2 * block, 2 * block) - pair * 2 * local
        names.append(name)
        matches = jnp.arange(2 * local, dtype=jnp.int32)[:, None] == name[None, :]
        drops.append(jnp.where(jnp.any(matches, axis=1), 0.0, 1.0).astype(jnp.bfloat16))
    names = jnp.stack(names)[:, :, None]
    drop = jnp.concatenate(drops).reshape(4, 1, local)

    n_blocks = n_wide // 4
    product_flops = 2 * total_rows * 4 * local * quarter
    shares = call(
        residual_kernel,
        jax.ShapeDtypeStruct((2, total_rows // 2, quarter), jnp.bfloat16),
        [SMEM] + [VMEM] * 7,
        product_flops,
        4 * total_rows * quarter,
    )(slot.reshape(1), hidden, other, drop, *downs)
    shares = shares.reshape(n_blocks, total_rows // n_blocks, quarter)
    strides = stride_groups()
    shares = lax.all_to_all(shares, "wide", 0, 0, axis_index_groups=strides)
    pieces = call(piece_kernel, jax.ShapeDtypeStruct(shares.shape, jnp.bfloat16), [VMEM], 0, 4 * total_rows * quarter)(shares)
    rounded = lax.all_to_all(pieces, "wide", 0, 0, axis_index_groups=strides).reshape(total_rows, quarter)

    chosen = call(
        select_kernel,
        jax.ShapeDtypeStruct((2, 2 * block, total_rows), jnp.bfloat16),
        [VMEM] * 3,
        4 * total_rows * local * 4 * block,
        4 * total_rows * local,
    )(names, hidden, other)
    factor = 1.0 / math.sqrt(total_rows)
    grad = call(
        functools.partial(gradient_kernel, factor),
        jax.ShapeDtypeStruct((4, block + 16, quarter), jnp.bfloat16),
        [VMEM] * 2,
        2 * total_rows * 4 * block * quarter,
        4 * total_rows * quarter,
    )(chosen, rounded)
    swapped = lax.all_to_all(grad, "wide", 0, 0, axis_index_groups=blocks)
    grad, errors = call(
        interleave_kernel,
        (
            jax.ShapeDtypeStruct((block, 4 * quarter), jnp.bfloat16),
            jax.ShapeDtypeStruct((n_tok, 8, 128), jnp.float32),
        ),
        [VMEM],
        0,
        4 * block * quarter,
    )(swapped)
    loss = jnp.sum(lax.all_to_all(errors, "tok", 0, 0)) / (total_rows * D)
    return (loss.reshape(1), grad[None])


def solution(mesh):
    in_specs = (
        P("wide", "tok"),
        P("tok"),
        P("tok", "wide"),
        P("tok", "wide"),
        P("wide", "tok"),
        P("var", None),
    )
    out_specs = (P("var"), P("var", "wide", "tok"))
    return jax.shard_map(
        per_device, mesh=mesh, in_specs=in_specs, out_specs=out_specs, check_vma=False
    )
```

```python
import functools
import math

import jax
import jax.numpy as jnp
from jax import lax
from jax.experimental import pallas as pl
from jax.experimental.pallas import tpu as pltpu
from jax.sharding import PartitionSpec as P

D = 8192
SIDE = 8


def block_groups():
    return [
        [(2 * a + i) * SIDE + 2 * b + j for i in range(2) for j in range(2)]
        for a in range(SIDE // 2)
        for b in range(SIDE // 2)
    ]


def stride_groups():
    return [
        [(2 * a + i) * SIDE + 2 * b + j for a in range(SIDE // 2) for b in range(SIDE // 2)]
        for i in range(2)
        for j in range(2)
    ]


VMEM = pl.BlockSpec(memory_space=pltpu.VMEM)
SMEM = pl.BlockSpec(memory_space=pltpu.SMEM)
HBM = pl.BlockSpec(memory_space=pltpu.HBM)


def call(kernel, out_shape, in_specs, flops, size, scratch=()):
    out_specs = jax.tree.map(lambda _: VMEM, out_shape)
    return pl.pallas_call(
        kernel,
        out_shape=out_shape,
        in_specs=in_specs,
        out_specs=out_specs,
        scratch_shapes=list(scratch),
        compiler_params=pltpu.CompilerParams(vmem_limit_bytes=16 * 1024 * 1024),
        cost_estimate=pl.CostEstimate(flops=flops, bytes_accessed=size, transcendentals=0),
    )


def spread_kernel(place_ref, tokens_ref, out_ref):
    width = out_ref.shape[2]
    tokens = tokens_ref[...].astype(jnp.float32)
    left, right = tokens[:, :width], tokens[:, width:]
    odd = place_ref[1] == 1
    first = jnp.where(odd, right, left)
    second = jnp.where(odd, left, right)
    upper = lax.broadcasted_iota(jnp.int32, first.shape, 0) < 4
    low = jnp.where(upper, first, pltpu.roll(second, 4, 0))
    high = jnp.where(upper, pltpu.roll(first, 4, 0), second)
    piece = jnp.where(place_ref[0] == 0, low, high).astype(out_ref.dtype)
    for i in range(out_ref.shape[0]):
        out_ref[i] = piece


def parent_kernel(tokens_ref, gain_ref, gate_hbm, up_hbm, out_ref, rows_ref, gate_ref, up_ref, sems):
    copies = [
        pltpu.make_async_copy(src, dst, sems.at[i])
        for i, (src, dst) in enumerate(((gate_hbm, gate_ref), (up_hbm, up_ref)))
    ]
    for copy in copies:
        copy.start()
    n_shards, _, width = tokens_ref.shape
    local = gate_ref.shape[0]
    lanes = out_ref.shape[1] // 2
    step = 16
    squares = []
    for i in range(0, n_shards, step):
        part = tokens_ref[i : i + step].astype(jnp.float32).reshape(step // 2, 2, 8, width)
        even, odd = part[:, 0], part[:, 1]
        upper = lax.broadcasted_iota(jnp.int32, even.shape, 1) < 4
        left = jnp.where(upper, even, odd)
        right = jnp.where(upper, odd, even)
        rows = slice(i * 4, (i + step) * 4)
        left = left.reshape(step * 4, width)
        right = pltpu.roll(right, 4, 1).reshape(step * 4, width)
        squares.append(jnp.sum(left * left + right * right, axis=1, keepdims=True))
        rows_ref[rows, :width] = (left * gain_ref[:, :width]).astype(rows_ref.dtype)
        rows_ref[rows, width:] = (right * gain_ref[:, width:]).astype(rows_ref.dtype)
    squares = jnp.concatenate(squares, axis=0)
    hi = squares.astype(jnp.bfloat16).astype(jnp.float32)
    contract = (((1,), (1,)), ((), ()))
    copies[0].wait()
    gate = lax.dot_general(rows_ref[...], gate_ref[...], contract, preferred_element_type=jnp.float32)
    copies[1].wait()
    up = lax.dot_general(rows_ref[...], up_ref[...], contract, preferred_element_type=jnp.float32)
    lane = lax.broadcasted_iota(jnp.int32, (squares.shape[0], lanes - local), 1)
    extra = jnp.where(lane == 0, hi, jnp.where(lane == 1, squares - hi, 0.0))
    out_ref[:, :local] = gate.astype(out_ref.dtype)
    out_ref[:, local:lanes] = extra.astype(out_ref.dtype)
    out_ref[:, lanes : lanes + local] = up.astype(out_ref.dtype)
    out_ref[:, lanes + local :] = jnp.zeros_like(extra).astype(out_ref.dtype)


def residual_kernel(slot_ref, own_hbm, other_hbm, drop_ref, down0, down1, down2, down3, out_ref, own_ref, other_ref, down_ref, sems):
    slot = slot_ref[0]
    local = down_ref.shape[1]
    copies = [pltpu.make_async_copy(own_hbm, own_ref, sems.at[0])]
    for k, down in enumerate((down0, down1, down2, down3)):
        copies.append(pltpu.make_async_copy(down, down_ref.at[k], sems.at[1 + k]))
    copies.append(pltpu.make_async_copy(other_hbm, other_ref, sems.at[5]))
    for copy in copies:
        copy.start()
    copies[0].wait()
    for half, hidden_ref in enumerate((own_ref, other_ref)):
        if half == 1:
            copies[5].wait()
        total = None
        for k in range(4):
            if half == 0:
                copies[1 + k].wait()
            index = slot ^ k
            units = hidden_ref[index][:, :local] * drop_ref[index]
            term = jnp.dot(units, down_ref[k], preferred_element_type=jnp.float32)
            total = term if total is None else total + term
        out_ref[half] = (-total).astype(out_ref.dtype)


def select_kernel(pair, names_ref, own_ref, other_ref, out_ref):
    rows = own_ref.shape[1]
    count = names_ref.shape[0]
    local = count
    names = names_ref[...]
    for half, hidden_ref in enumerate((own_ref, other_ref)):
        total = None
        for i in range(2):
            units = lax.broadcasted_iota(jnp.int32, (count, local), 1) + i * local
            picker = jnp.where(units == names, 1.0, 0.0).astype(jnp.bfloat16)
            term = lax.dot_general(
                picker,
                hidden_ref[2 * pair + i][:, :local],
                (((1,), (1,)), ((), ())),
                preferred_element_type=jnp.float32,
            )
            total = term if total is None else total + term
        out_ref[:, half * rows : (half + 1) * rows] = total.astype(out_ref.dtype)


def hidden_kernel(local, sums_ref, out_ref):
    total = sums_ref[0].astype(jnp.float32)
    for i in range(1, sums_ref.shape[0]):
        total = total + sums_ref[i].astype(jnp.float32)
    squares = total[:, local : local + 1] + total[:, local + 1 : local + 2]
    scale = lax.rsqrt(squares / D + 1e-05)
    half = total.shape[1] // 2
    gate = total[:, :half] * scale
    up = total[:, half:] * scale
    hidden = (gate / (1.0 + jnp.exp(-gate)) * up).astype(out_ref.dtype)
    for i in range(out_ref.shape[0]):
        out_ref[i] = hidden


def piece_kernel(shares_ref, out_ref):
    total = shares_ref[0].astype(jnp.float32)
    for i in range(1, shares_ref.shape[0]):
        total = total + shares_ref[i].astype(jnp.float32)
    piece = total.astype(out_ref.dtype)
    for i in range(out_ref.shape[0]):
        out_ref[i] = piece


def gradient_kernel(factor, first_ref, second_ref, rounded_ref, out_ref, error_ref):
    rounded = rounded_ref[...]
    block = out_ref.shape[1]
    for pair, chosen_ref in enumerate((first_ref, second_ref)):
        product = jnp.dot(chosen_ref[...], rounded, preferred_element_type=jnp.float32) * factor
        for i in range(2):
            out_ref[2 * pair + i] = product[i * block : (i + 1) * block].astype(out_ref.dtype)
    errors = rounded.astype(jnp.float32)
    columns = jnp.sum(errors * errors, axis=0, keepdims=True)
    lanes = columns[:, :128]
    for i in range(1, columns.shape[1] // 128):
        lanes = lanes + columns[:, i * 128 : (i + 1) * 128]
    error_ref[...] = lanes


def interleave_kernel(in_ref, out_ref):
    width = in_ref.shape[2]
    for i in range(in_ref.shape[0]):
        out_ref[:, i * width : (i + 1) * width] = in_ref[i]


def per_device(tokens, norm_gain, gate_parent, up_parent, down_parent, kept):
    n_wide = lax.axis_size("wide")
    n_tok = lax.axis_size("tok")
    core = lax.axis_index("var")
    wide = lax.axis_index("wide")
    row, col = wide // SIDE, wide % SIDE
    slot = (row % 2) * 2 + col % 2
    local = gate_parent.shape[1]
    width = tokens.shape[1]
    blocks = block_groups()

    half = tokens.shape[0] // 2
    pieces = call(
        spread_kernel,
        jax.ShapeDtypeStruct((n_wide, 2 * half, width // 2), jnp.bfloat16),
        [SMEM, VMEM],
        0,
        2 * n_wide * half * width,
    )(jnp.stack([core, wide % 2]), tokens)
    gathered = lax.all_to_all(pieces, "wide", 0, 0)

    quarter = down_parent.shape[1] // 4
    downs = [lax.dynamic_slice_in_dim(down_parent, (slot ^ k) * quarter, quarter, 1) for k in range(4)]
    for k in range(1, 4):
        perm = [(w, w ^ ((k // 2) * SIDE + k % 2)) for w in range(n_wide)]
        downs[k] = lax.ppermute(downs[k], "wide", perm)

    pad = (-local) % 128
    partial = call(
        parent_kernel,
        jax.ShapeDtypeStruct((n_wide * half, 2 * (local + pad)), jnp.bfloat16),
        [VMEM] * 2 + [HBM] * 2,
        4 * n_wide * half * width * local,
        8 * width * local,
        [
            pltpu.VMEM((n_wide * half, width), jnp.bfloat16),
            pltpu.VMEM((local, width), jnp.bfloat16),
            pltpu.VMEM((local, width), jnp.bfloat16),
            pltpu.SemaphoreType.DMA((2,)),
        ],
    )(gathered, norm_gain.reshape(1, width), gate_parent.T, up_parent.T)
    rows = n_wide * half // n_tok

    scattered = lax.all_to_all(partial.reshape(n_tok, rows, 2 * (local + pad)), "tok", 0, 0)
    scattered, *downs = lax.optimization_barrier((scattered, *downs))
    hidden = call(
        functools.partial(hidden_kernel, local),
        jax.ShapeDtypeStruct((4 * n_tok, rows, local + pad), jnp.bfloat16),
        [VMEM],
        0,
        16 * rows * local,
    )(scattered)

    groups = [[t * n_wide + w for w in block for t in range(n_tok)] for block in blocks]
    hidden = lax.all_to_all(hidden, ("tok", "wide"), 0, 0, axis_index_groups=groups)
    var_kept = kept[0]
    block = var_kept.shape[0] // n_wide
    names = []
    drops = []
    for i in range(2):
        pair = (row // 2 * 2 + i) * (SIDE // 2) + col // 2
        name = lax.dynamic_slice_in_dim(var_kept, pair * 2 * block, 2 * block) - pair * 2 * local
        names.append(name)
        matches = jnp.arange(2 * local, dtype=jnp.int32)[:, None] == name[None, :]
        drops.append(jnp.where(jnp.any(matches, axis=1), 0.0, 1.0).astype(jnp.bfloat16))
    names = [name[:, None] for name in names]
    drop = jnp.concatenate(drops).reshape(4, 1, local)
    hidden, drop, *names = lax.optimization_barrier((hidden, drop, *names))
    hidden = hidden.reshape(4, n_tok * rows, local + pad)
    other = lax.ppermute(hidden, "var", [(0, 1), (1, 0)])
    total_rows = 2 * n_tok * rows

    n_blocks = n_wide // 4
    product_flops = 2 * total_rows * 4 * local * quarter
    shares = call(
        residual_kernel,
        jax.ShapeDtypeStruct((2, total_rows // 2, quarter), jnp.bfloat16),
        [SMEM, HBM, HBM, VMEM] + [HBM] * 4,
        product_flops,
        4 * total_rows * quarter,
        [
            pltpu.VMEM(hidden.shape, jnp.bfloat16),
            pltpu.VMEM(hidden.shape, jnp.bfloat16),
            pltpu.VMEM((4, local, quarter), jnp.bfloat16),
            pltpu.SemaphoreType.DMA((6,)),
        ],
    )(slot.reshape(1), hidden, other, drop, *downs)
    shares = shares.reshape(n_blocks, total_rows // n_blocks, quarter)
    strides = stride_groups()
    chosen = [
        call(
            functools.partial(select_kernel, pair),
            jax.ShapeDtypeStruct((2 * block, total_rows), jnp.bfloat16),
            [VMEM] * 3,
            2 * total_rows * local * 4 * block,
            2 * total_rows * local,
        )(names[pair], hidden, other)
        for pair in range(2)
    ]
    shares = lax.all_to_all(shares, "wide", 0, 0, axis_index_groups=strides)
    shares, chosen[0] = lax.optimization_barrier((shares, chosen[0]))
    pieces = call(piece_kernel, jax.ShapeDtypeStruct(shares.shape, jnp.bfloat16), [VMEM], 0, 4 * total_rows * quarter)(shares)
    rounded = lax.all_to_all(pieces, "wide", 0, 0, axis_index_groups=strides).reshape(total_rows, quarter)

    factor = 1.0 / math.sqrt(total_rows)
    grad, errors = call(
        functools.partial(gradient_kernel, factor),
        (
            jax.ShapeDtypeStruct((4, block, quarter), jnp.bfloat16),
            jax.ShapeDtypeStruct((1, 128), jnp.float32),
        ),
        [VMEM] * 3,
        2 * total_rows * 4 * block * quarter,
        4 * total_rows * quarter,
    )(*chosen, rounded)

    errors = lax.psum(errors, "tok")
    errors = jnp.broadcast_to(errors, (4, 8, 128))
    swapped = lax.all_to_all(grad, "wide", 0, 0, axis_index_groups=blocks)
    swapped, errors = lax.optimization_barrier((swapped, errors))
    errors = lax.all_to_all(errors, "wide", 0, 0, axis_index_groups=blocks)
    loss = jnp.sum(errors[:, 0]) / (total_rows * D)
    grad = call(
        interleave_kernel,
        jax.ShapeDtypeStruct((block, 4 * quarter), jnp.bfloat16),
        [VMEM],
        0,
        4 * block * quarter,
    )(swapped)
    return (loss.reshape(1), grad[None])


def solution(mesh):
    in_specs = (
        P("wide", "tok"),
        P("tok"),
        P("tok", "wide"),
        P("tok", "wide"),
        P("wide", "tok"),
        P("var", None),
    )
    out_specs = (P("var"), P("var", "wide", "tok"))
    return jax.shard_map(
        per_device, mesh=mesh, in_specs=in_specs, out_specs=out_specs, check_vma=False
    )
```

```python
import functools
import math

import jax
import jax.numpy as jnp
from jax import lax
from jax.experimental import pallas as pl
from jax.experimental.pallas import tpu as pltpu
from jax.sharding import PartitionSpec as P

D = 8192
SIDE = 8


def block_groups():
    return [
        [(2 * a + i) * SIDE + 2 * b + j for i in range(2) for j in range(2)]
        for a in range(SIDE // 2)
        for b in range(SIDE // 2)
    ]


def stride_groups():
    return [
        [(2 * a + i) * SIDE + 2 * b + j for a in range(SIDE // 2) for b in range(SIDE // 2)]
        for i in range(2)
        for j in range(2)
    ]


VMEM = pl.BlockSpec(memory_space=pltpu.VMEM)
SMEM = pl.BlockSpec(memory_space=pltpu.SMEM)


def call(kernel, out_shape, in_specs, flops, size, scratch=()):
    out_specs = jax.tree.map(lambda _: VMEM, out_shape)
    return pl.pallas_call(
        kernel,
        out_shape=out_shape,
        in_specs=in_specs,
        out_specs=out_specs,
        scratch_shapes=list(scratch),
        compiler_params=pltpu.CompilerParams(vmem_limit_bytes=16 * 1024 * 1024),
        cost_estimate=pl.CostEstimate(flops=flops, bytes_accessed=size, transcendentals=0),
    )


def spread_kernel(place_ref, tokens_ref, out_ref):
    width = out_ref.shape[2]
    tokens = tokens_ref[...].astype(jnp.float32)
    left, right = tokens[:, :width], tokens[:, width:]
    odd = place_ref[1] == 1
    first = jnp.where(odd, right, left)
    second = jnp.where(odd, left, right)
    upper = lax.broadcasted_iota(jnp.int32, first.shape, 0) < 4
    low = jnp.where(upper, first, pltpu.roll(second, 4, 0))
    high = jnp.where(upper, pltpu.roll(first, 4, 0), second)
    piece = jnp.where(place_ref[0] == 0, low, high).astype(out_ref.dtype)
    for i in range(out_ref.shape[0]):
        out_ref[i] = piece


def parent_kernel(tokens_ref, gain_ref, weights_ref, out_ref, rows_ref):
    n_shards, _, width = tokens_ref.shape
    local = weights_ref.shape[0] // 2
    lanes = out_ref.shape[1] // 2
    step = 16
    squares = []
    for i in range(0, n_shards, step):
        part = tokens_ref[i : i + step].astype(jnp.float32).reshape(step // 2, 2, 8, width)
        even, odd = part[:, 0], part[:, 1]
        upper = lax.broadcasted_iota(jnp.int32, even.shape, 1) < 4
        left = jnp.where(upper, even, odd)
        right = jnp.where(upper, odd, even)
        rows = slice(i * 4, (i + step) * 4)
        left = left.reshape(step * 4, width)
        right = pltpu.roll(right, 4, 1).reshape(step * 4, width)
        squares.append(jnp.sum(left * left + right * right, axis=1, keepdims=True))
        rows_ref[rows, :width] = (left * gain_ref[:, :width]).astype(rows_ref.dtype)
        rows_ref[rows, width:] = (right * gain_ref[:, width:]).astype(rows_ref.dtype)
    squares = jnp.concatenate(squares, axis=0)
    hi = squares.astype(jnp.bfloat16).astype(jnp.float32)
    contract = (((1,), (1,)), ((), ()))
    gate = lax.dot_general(rows_ref[...], weights_ref[:local], contract, preferred_element_type=jnp.float32)
    up = lax.dot_general(rows_ref[...], weights_ref[local:], contract, preferred_element_type=jnp.float32)
    lane = lax.broadcasted_iota(jnp.int32, (squares.shape[0], lanes - local), 1)
    extra = jnp.where(lane == 0, hi, jnp.where(lane == 1, squares - hi, 0.0))
    out_ref[:, :local] = gate.astype(out_ref.dtype)
    out_ref[:, local:lanes] = extra.astype(out_ref.dtype)
    out_ref[:, lanes : lanes + local] = up.astype(out_ref.dtype)
    out_ref[:, lanes + local :] = jnp.zeros_like(extra).astype(out_ref.dtype)


def residual_kernel(slot_ref, own_ref, other_ref, drop_ref, down0, down1, down2, down3, out_ref):
    slot = slot_ref[0]
    downs = (down0, down1, down2, down3)
    local = down0.shape[0]
    for half, hidden_ref in enumerate((own_ref, other_ref)):
        total = None
        for k in range(4):
            index = slot ^ k
            units = hidden_ref[index][:, :local] * drop_ref[index]
            term = jnp.dot(units, downs[k][...], preferred_element_type=jnp.float32)
            total = term if total is None else total + term
        out_ref[half] = (-total).astype(out_ref.dtype)


def select_kernel(names_ref, own_ref, other_ref, out_ref):
    rows = own_ref.shape[1]
    count = names_ref.shape[1]
    local = count
    for pair in range(2):
        names = names_ref[pair]
        for half, hidden_ref in enumerate((own_ref, other_ref)):
            total = None
            for i in range(2):
                units = lax.broadcasted_iota(jnp.int32, (count, local), 1) + i * local
                picker = jnp.where(units == names, 1.0, 0.0).astype(jnp.bfloat16)
                term = lax.dot_general(
                    picker,
                    hidden_ref[2 * pair + i][:, :local],
                    (((1,), (1,)), ((), ())),
                    preferred_element_type=jnp.float32,
                )
                total = term if total is None else total + term
            out_ref[pair, :, half * rows : (half + 1) * rows] = total.astype(out_ref.dtype)


def hidden_kernel(local, sums_ref, out_ref):
    total = sums_ref[0].astype(jnp.float32)
    for i in range(1, sums_ref.shape[0]):
        total = total + sums_ref[i].astype(jnp.float32)
    squares = total[:, local : local + 1] + total[:, local + 1 : local + 2]
    scale = lax.rsqrt(squares / D + 1e-05)
    half = total.shape[1] // 2
    gate = total[:, :half] * scale
    up = total[:, half:] * scale
    hidden = (gate / (1.0 + jnp.exp(-gate)) * up).astype(out_ref.dtype)
    for i in range(out_ref.shape[0]):
        out_ref[i] = hidden


def piece_kernel(shares_ref, out_ref):
    total = shares_ref[0].astype(jnp.float32)
    for i in range(1, shares_ref.shape[0]):
        total = total + shares_ref[i].astype(jnp.float32)
    piece = total.astype(out_ref.dtype)
    for i in range(out_ref.shape[0]):
        out_ref[i] = piece


def gradient_kernel(factor, slot_ref, chosen_ref, rounded_ref, out0, out1, out2, out3, error_ref, rows_ref):
    slot = slot_ref[0]
    rounded = rounded_ref[...]
    block = out0.shape[0]
    for pair in range(2):
        product = jnp.dot(chosen_ref[pair], rounded, preferred_element_type=jnp.float32) * factor
        for i in range(2):
            rows_ref[2 * pair + i] = product[i * block : (i + 1) * block].astype(rows_ref.dtype)
    for k, out_ref in enumerate((out0, out1, out2, out3)):
        out_ref[...] = rows_ref[slot ^ k]
    errors = rounded.astype(jnp.float32)
    columns = jnp.sum(errors * errors, axis=0, keepdims=True)
    lanes = columns[:, :128]
    for i in range(1, columns.shape[1] // 128):
        lanes = lanes + columns[:, i * 128 : (i + 1) * 128]
    line = lax.broadcasted_iota(jnp.int32, (8, 128), 0)
    lanes = jnp.where(line == 0, lanes, 0.0)
    for i in range(error_ref.shape[0]):
        error_ref[i] = lanes


def interleave_kernel(slot_ref, in0, in1, in2, in3, out_ref):
    slot = slot_ref[0]
    width = in0.shape[1]
    for k, in_ref in enumerate((in0, in1, in2, in3)):
        start = pl.multiple_of((slot ^ k) * width, 128)
        out_ref[:, pl.ds(start, width)] = in_ref[...]


def per_device(tokens, norm_gain, gate_parent, up_parent, down_parent, kept):
    n_wide = lax.axis_size("wide")
    n_tok = lax.axis_size("tok")
    core = lax.axis_index("var")
    wide = lax.axis_index("wide")
    row, col = wide // SIDE, wide % SIDE
    slot = (row % 2) * 2 + col % 2
    local = gate_parent.shape[1]
    width = tokens.shape[1]
    blocks = block_groups()

    half = tokens.shape[0] // 2
    pieces = call(
        spread_kernel,
        jax.ShapeDtypeStruct((n_wide, 2 * half, width // 2), jnp.bfloat16),
        [SMEM, VMEM],
        0,
        2 * n_wide * half * width,
    )(jnp.stack([core, wide % 2]), tokens)
    gathered = lax.all_to_all(pieces, "wide", 0, 0)

    quarter = down_parent.shape[1] // 4
    downs = [lax.dynamic_slice_in_dim(down_parent, (slot ^ k) * quarter, quarter, 1) for k in range(4)]
    for k in range(1, 4):
        perm = [(w, w ^ ((k // 2) * SIDE + k % 2)) for w in range(n_wide)]
        downs[k] = lax.ppermute(downs[k], "wide", perm)

    weights = jnp.concatenate([gate_parent.T, up_parent.T], axis=0)
    gathered, weights = lax.optimization_barrier((gathered, weights))
    pad = (-local) % 128
    partial = call(
        parent_kernel,
        jax.ShapeDtypeStruct((n_wide * half, 2 * (local + pad)), jnp.bfloat16),
        [VMEM] * 3,
        4 * n_wide * half * width * local,
        8 * width * local,
        [pltpu.VMEM((n_wide * half, width), jnp.bfloat16)],
    )(gathered, norm_gain.reshape(1, width), weights)
    rows = n_wide * half // n_tok

    scattered = lax.all_to_all(partial.reshape(n_tok, rows, 2 * (local + pad)), "tok", 0, 0)
    scattered, *downs = lax.optimization_barrier((scattered, *downs))
    hidden = call(
        functools.partial(hidden_kernel, local),
        jax.ShapeDtypeStruct((4 * n_tok, rows, local + pad), jnp.bfloat16),
        [VMEM],
        0,
        16 * rows * local,
    )(scattered)

    groups = [[t * n_wide + w for w in block for t in range(n_tok)] for block in blocks]
    hidden = lax.all_to_all(hidden, ("tok", "wide"), 0, 0, axis_index_groups=groups)
    hidden = hidden.reshape(4, n_tok * rows, local + pad)
    other = lax.ppermute(hidden, "var", [(0, 1), (1, 0)])
    total_rows = 2 * n_tok * rows

    var_kept = kept[0]
    block = var_kept.shape[0] // n_wide
    names = []
    drops = []
    for i in range(2):
        pair = (row // 2 * 2 + i) * (SIDE // 2) + col // 2
        name = lax.dynamic_slice_in_dim(var_kept, pair * 2 * block, 2 * block) - pair * 2 * local
        names.append(name)
        matches = jnp.arange(2 * local, dtype=jnp.int32)[:, None] == name[None, :]
        drops.append(jnp.where(jnp.any(matches, axis=1), 0.0, 1.0).astype(jnp.bfloat16))
    names = jnp.stack(names)[:, :, None]
    drop = jnp.concatenate(drops).reshape(4, 1, local)

    n_blocks = n_wide // 4
    product_flops = 2 * total_rows * 4 * local * quarter
    shares = call(
        residual_kernel,
        jax.ShapeDtypeStruct((2, total_rows // 2, quarter), jnp.bfloat16),
        [SMEM] + [VMEM] * 7,
        product_flops,
        4 * total_rows * quarter,
    )(slot.reshape(1), hidden, other, drop, *downs)
    shares = shares.reshape(n_blocks, total_rows // n_blocks, quarter)
    strides = stride_groups()
    shares = lax.all_to_all(shares, "wide", 0, 0, axis_index_groups=strides)
    pieces = call(piece_kernel, jax.ShapeDtypeStruct(shares.shape, jnp.bfloat16), [VMEM], 0, 4 * total_rows * quarter)(shares)
    rounded = lax.all_to_all(pieces, "wide", 0, 0, axis_index_groups=strides).reshape(total_rows, quarter)

    chosen = call(
        select_kernel,
        jax.ShapeDtypeStruct((2, 2 * block, total_rows), jnp.bfloat16),
        [VMEM] * 3,
        4 * total_rows * local * 4 * block,
        4 * total_rows * local,
    )(names, hidden, other)
    factor = 1.0 / math.sqrt(total_rows)
    *grads, errors = call(
        functools.partial(gradient_kernel, factor),
        (
            *[jax.ShapeDtypeStruct((block, quarter), jnp.bfloat16)] * 4,
            jax.ShapeDtypeStruct((4 * n_tok, 8, 128), jnp.float32),
        ),
        [SMEM, VMEM, VMEM],
        2 * total_rows * 4 * block * quarter,
        4 * total_rows * quarter,
        [pltpu.VMEM((4, block, quarter), jnp.bfloat16)],
    )(slot.reshape(1), chosen, rounded)
    errors = lax.all_to_all(errors, ("tok", "wide"), 0, 0, axis_index_groups=groups)
    loss = jnp.sum(errors) / (total_rows * D)
    for k in range(1, 4):
        perm = [(w, w ^ ((k // 2) * SIDE + k % 2)) for w in range(n_wide)]
        grads[k] = lax.ppermute(grads[k], "wide", perm)
    grad = call(
        interleave_kernel,
        jax.ShapeDtypeStruct((block, 4 * quarter), jnp.bfloat16),
        [SMEM] + [VMEM] * 4,
        0,
        4 * block * quarter,
    )(slot.reshape(1), *grads)
    return (loss.reshape(1), grad[None])


def solution(mesh):
    in_specs = (
        P("wide", "tok"),
        P("tok"),
        P("tok", "wide"),
        P("tok", "wide"),
        P("wide", "tok"),
        P("var", None),
    )
    out_specs = (P("var"), P("var", "wide", "tok"))
    return jax.shard_map(
        per_device, mesh=mesh, in_specs=in_specs, out_specs=out_specs, check_vma=False
    )
```

```python
import functools
import math

import jax
import jax.numpy as jnp
from jax import lax
from jax.experimental import pallas as pl
from jax.experimental.pallas import tpu as pltpu
from jax.sharding import PartitionSpec as P

D = 8192
SIDE = 8


def block_groups():
    return [
        [(2 * a + i) * SIDE + 2 * b + j for i in range(2) for j in range(2)]
        for a in range(SIDE // 2)
        for b in range(SIDE // 2)
    ]


def stride_groups():
    return [
        [(2 * a + i) * SIDE + 2 * b + j for a in range(SIDE // 2) for b in range(SIDE // 2)]
        for i in range(2)
        for j in range(2)
    ]


VMEM = pl.BlockSpec(memory_space=pltpu.VMEM)
SMEM = pl.BlockSpec(memory_space=pltpu.SMEM)
ANY = pl.BlockSpec(memory_space=pl.ANY)
COPIES = 8


def call(kernel, out_shape, in_specs, flops, size, scratch=(), out_spec=None):
    out_specs = jax.tree.map(lambda _: out_spec or VMEM, out_shape)
    return pl.pallas_call(
        kernel,
        out_shape=out_shape,
        in_specs=in_specs,
        out_specs=out_specs,
        scratch_shapes=list(scratch),
        compiler_params=pltpu.CompilerParams(vmem_limit_bytes=16 * 1024 * 1024),
        cost_estimate=pl.CostEstimate(flops=flops, bytes_accessed=size, transcendentals=0),
    )


def repeat(piece, out_ref, held_ref, sems):
    count = held_ref.shape[0]
    for i in range(count):
        held_ref[i] = piece
    copies = [
        pltpu.make_async_copy(held_ref, out_ref.at[pl.ds(i * count, count)], sems.at[i])
        for i in range(COPIES)
    ]
    for copy in copies:
        copy.start()
    for copy in copies:
        copy.wait()


def repeated(kernel, out_shape, in_specs):
    count = out_shape.shape[0] // COPIES
    size = 4 * math.prod(out_shape.shape)
    scratch = [
        pltpu.VMEM((count,) + out_shape.shape[1:], out_shape.dtype),
        pltpu.SemaphoreType.DMA((COPIES,)),
    ]
    return call(kernel, out_shape, in_specs, 0, size, scratch, ANY)


def spread_kernel(place_ref, tokens_ref, out_ref, held_ref, sems):
    width = out_ref.shape[2]
    tokens = tokens_ref[...].astype(jnp.float32)
    left, right = tokens[:, :width], tokens[:, width:]
    odd = place_ref[1] == 1
    first = jnp.where(odd, right, left)
    second = jnp.where(odd, left, right)
    upper = lax.broadcasted_iota(jnp.int32, first.shape, 0) < 4
    low = jnp.where(upper, first, pltpu.roll(second, 4, 0))
    high = jnp.where(upper, pltpu.roll(first, 4, 0), second)
    piece = jnp.where(place_ref[0] == 0, low, high).astype(out_ref.dtype)
    repeat(piece, out_ref, held_ref, sems)


def parent_kernel(tokens_ref, gain_ref, weights_ref, out_ref, rows_ref):
    n_shards, _, width = tokens_ref.shape
    local = weights_ref.shape[0] // 2
    lanes = out_ref.shape[1] // 2
    step = 16
    squares = []
    for i in range(0, n_shards, step):
        part = tokens_ref[i : i + step].astype(jnp.float32).reshape(step // 2, 2, 8, width)
        even, odd = part[:, 0], part[:, 1]
        upper = lax.broadcasted_iota(jnp.int32, even.shape, 1) < 4
        left = jnp.where(upper, even, odd)
        right = jnp.where(upper, odd, even)
        rows = slice(i * 4, (i + step) * 4)
        left = left.reshape(step * 4, width)
        right = pltpu.roll(right, 4, 1).reshape(step * 4, width)
        squares.append(jnp.sum(left * left + right * right, axis=1, keepdims=True))
        rows_ref[rows, :width] = (left * gain_ref[:, :width]).astype(rows_ref.dtype)
        rows_ref[rows, width:] = (right * gain_ref[:, width:]).astype(rows_ref.dtype)
    squares = jnp.concatenate(squares, axis=0)
    hi = squares.astype(jnp.bfloat16).astype(jnp.float32)
    contract = (((1,), (1,)), ((), ()))
    gate = lax.dot_general(rows_ref[...], weights_ref[:local], contract, preferred_element_type=jnp.float32)
    up = lax.dot_general(rows_ref[...], weights_ref[local:], contract, preferred_element_type=jnp.float32)
    lane = lax.broadcasted_iota(jnp.int32, (squares.shape[0], lanes - local), 1)
    extra = jnp.where(lane == 0, hi, jnp.where(lane == 1, squares - hi, 0.0))
    out_ref[:, :local] = gate.astype(out_ref.dtype)
    out_ref[:, local:lanes] = extra.astype(out_ref.dtype)
    out_ref[:, lanes : lanes + local] = up.astype(out_ref.dtype)
    out_ref[:, lanes + local :] = jnp.zeros_like(extra).astype(out_ref.dtype)


def residual_kernel(slot_ref, own_ref, other_ref, drop_ref, down0, down1, down2, down3, out_ref):
    slot = slot_ref[0]
    downs = (down0, down1, down2, down3)
    local = down0.shape[0]
    for half, hidden_ref in enumerate((own_ref, other_ref)):
        total = None
        for k in range(4):
            index = slot ^ k
            units = hidden_ref[index][:, :local] * drop_ref[index]
            term = jnp.dot(units, downs[k][...], preferred_element_type=jnp.float32)
            total = term if total is None else total + term
        out_ref[half] = (-total).astype(out_ref.dtype)


def select_kernel(names_ref, own_ref, other_ref, out_ref):
    rows = own_ref.shape[1]
    count = names_ref.shape[1]
    local = count
    for pair in range(2):
        names = names_ref[pair]
        for half, hidden_ref in enumerate((own_ref, other_ref)):
            total = None
            for i in range(2):
                units = lax.broadcasted_iota(jnp.int32, (count, local), 1) + i * local
                picker = jnp.where(units == names, 1.0, 0.0).astype(jnp.bfloat16)
                term = lax.dot_general(
                    picker,
                    hidden_ref[2 * pair + i][:, :local],
                    (((1,), (1,)), ((), ())),
                    preferred_element_type=jnp.float32,
                )
                total = term if total is None else total + term
            out_ref[pair, :, half * rows : (half + 1) * rows] = total.astype(out_ref.dtype)


def hidden_kernel(local, sums_ref, out_ref, held_ref, sems):
    total = sums_ref[0].astype(jnp.float32)
    for i in range(1, sums_ref.shape[0]):
        total = total + sums_ref[i].astype(jnp.float32)
    squares = total[:, local : local + 1] + total[:, local + 1 : local + 2]
    scale = lax.rsqrt(squares / D + 1e-05)
    half = total.shape[1] // 2
    gate = total[:, :half] * scale
    up = total[:, half:] * scale
    hidden = (gate / (1.0 + jnp.exp(-gate)) * up).astype(out_ref.dtype)
    repeat(hidden, out_ref, held_ref, sems)


def piece_kernel(shares_ref, out_ref, held_ref, sems):
    total = shares_ref[0].astype(jnp.float32)
    for i in range(1, shares_ref.shape[0]):
        total = total + shares_ref[i].astype(jnp.float32)
    repeat(total.astype(out_ref.dtype), out_ref, held_ref, sems)


def gradient_kernel(factor, slot_ref, chosen_ref, rounded_ref, out0, out1, out2, out3, error_ref, rows_ref):
    slot = slot_ref[0]
    rounded = rounded_ref[...]
    block = out0.shape[0]
    for pair in range(2):
        product = jnp.dot(chosen_ref[pair], rounded, preferred_element_type=jnp.float32) * factor
        for i in range(2):
            rows_ref[2 * pair + i] = product[i * block : (i + 1) * block].astype(rows_ref.dtype)
    for k, out_ref in enumerate((out0, out1, out2, out3)):
        out_ref[...] = rows_ref[slot ^ k]
    errors = rounded.astype(jnp.float32)
    columns = jnp.sum((errors * errors).reshape(-1, 16, errors.shape[1]), axis=0)
    lanes = columns[:, :128]
    for i in range(1, columns.shape[1] // 128):
        lanes = lanes + columns[:, i * 128 : (i + 1) * 128]
    for i in range(error_ref.shape[0]):
        error_ref[i] = lanes


def interleave_kernel(slot_ref, in0, in1, in2, in3, out_ref):
    slot = slot_ref[0]
    width = in0.shape[1]
    for k, in_ref in enumerate((in0, in1, in2, in3)):
        start = pl.multiple_of((slot ^ k) * width, 128)
        out_ref[:, pl.ds(start, width)] = in_ref[...]


def per_device(tokens, norm_gain, gate_parent, up_parent, down_parent, kept):
    n_wide = lax.axis_size("wide")
    n_tok = lax.axis_size("tok")
    core = lax.axis_index("var")
    wide = lax.axis_index("wide")
    row, col = wide // SIDE, wide % SIDE
    slot = (row % 2) * 2 + col % 2
    local = gate_parent.shape[1]
    width = tokens.shape[1]
    blocks = block_groups()

    half = tokens.shape[0] // 2
    pieces = repeated(
        spread_kernel,
        jax.ShapeDtypeStruct((n_wide, 2 * half, width // 2), jnp.bfloat16),
        [SMEM, VMEM],
    )(jnp.stack([core, wide % 2]), tokens)
    gathered = lax.all_to_all(pieces, "wide", 0, 0)

    quarter = down_parent.shape[1] // 4
    downs = [lax.dynamic_slice_in_dim(down_parent, (slot ^ k) * quarter, quarter, 1) for k in range(4)]
    for k in range(1, 4):
        perm = [(w, w ^ ((k // 2) * SIDE + k % 2)) for w in range(n_wide)]
        downs[k] = lax.ppermute(downs[k], "wide", perm)

    weights = jnp.concatenate([gate_parent.T, up_parent.T], axis=0)
    gathered, weights = lax.optimization_barrier((gathered, weights))
    pad = (-local) % 128
    partial = call(
        parent_kernel,
        jax.ShapeDtypeStruct((n_wide * half, 2 * (local + pad)), jnp.bfloat16),
        [VMEM] * 3,
        4 * n_wide * half * width * local,
        8 * width * local,
        [pltpu.VMEM((n_wide * half, width), jnp.bfloat16)],
    )(gathered, norm_gain.reshape(1, width), weights)
    rows = n_wide * half // n_tok

    scattered = lax.all_to_all(partial.reshape(n_tok, rows, 2 * (local + pad)), "tok", 0, 0)
    scattered, *downs = lax.optimization_barrier((scattered, *downs))
    hidden = repeated(
        functools.partial(hidden_kernel, local),
        jax.ShapeDtypeStruct((4 * n_tok, rows, local + pad), jnp.bfloat16),
        [VMEM],
    )(scattered)

    groups = [[t * n_wide + w for w in block for t in range(n_tok)] for block in blocks]
    hidden = lax.all_to_all(hidden, ("tok", "wide"), 0, 0, axis_index_groups=groups)
    hidden = hidden.reshape(4, n_tok * rows, local + pad)
    other = lax.ppermute(hidden, "var", [(0, 1), (1, 0)])
    total_rows = 2 * n_tok * rows

    var_kept = kept[0]
    block = var_kept.shape[0] // n_wide
    names = []
    drops = []
    for i in range(2):
        pair = (row // 2 * 2 + i) * (SIDE // 2) + col // 2
        name = lax.dynamic_slice_in_dim(var_kept, pair * 2 * block, 2 * block) - pair * 2 * local
        names.append(name)
        matches = jnp.arange(2 * local, dtype=jnp.int32)[:, None] == name[None, :]
        drops.append(jnp.where(jnp.any(matches, axis=1), 0.0, 1.0).astype(jnp.bfloat16))
    names = jnp.stack(names)[:, :, None]
    drop = jnp.concatenate(drops).reshape(4, 1, local)

    n_blocks = n_wide // 4
    product_flops = 2 * total_rows * 4 * local * quarter
    shares = call(
        residual_kernel,
        jax.ShapeDtypeStruct((2, total_rows // 2, quarter), jnp.bfloat16),
        [SMEM] + [VMEM] * 7,
        product_flops,
        4 * total_rows * quarter,
    )(slot.reshape(1), hidden, other, drop, *downs)
    shares = shares.reshape(n_blocks, total_rows // n_blocks, quarter)
    strides = stride_groups()
    shares = lax.all_to_all(shares, "wide", 0, 0, axis_index_groups=strides)
    pieces = repeated(piece_kernel, jax.ShapeDtypeStruct(shares.shape, jnp.bfloat16), [VMEM])(shares)
    rounded = lax.all_to_all(pieces, "wide", 0, 0, axis_index_groups=strides).reshape(total_rows, quarter)

    chosen = call(
        select_kernel,
        jax.ShapeDtypeStruct((2, 2 * block, total_rows), jnp.bfloat16),
        [VMEM] * 3,
        4 * total_rows * local * 4 * block,
        4 * total_rows * local,
    )(names, hidden, other)
    factor = 1.0 / math.sqrt(total_rows)
    *grads, errors = call(
        functools.partial(gradient_kernel, factor),
        (
            *[jax.ShapeDtypeStruct((block, quarter), jnp.bfloat16)] * 4,
            jax.ShapeDtypeStruct((4 * n_tok, 16, 128), jnp.float32),
        ),
        [SMEM, VMEM, VMEM],
        2 * total_rows * 4 * block * quarter,
        4 * total_rows * quarter,
        [pltpu.VMEM((4, block, quarter), jnp.bfloat16)],
    )(slot.reshape(1), chosen, rounded)
    errors = lax.all_to_all(errors, ("tok", "wide"), 0, 0, axis_index_groups=groups)
    loss = jnp.sum(errors) / (total_rows * D)
    for k in range(1, 4):
        perm = [(w, w ^ ((k // 2) * SIDE + k % 2)) for w in range(n_wide)]
        grads[k] = lax.ppermute(grads[k], "wide", perm)
    grad = call(
        interleave_kernel,
        jax.ShapeDtypeStruct((block, 4 * quarter), jnp.bfloat16),
        [SMEM] + [VMEM] * 4,
        0,
        4 * block * quarter,
    )(slot.reshape(1), *grads)
    return (loss.reshape(1), grad[None])


def solution(mesh):
    in_specs = (
        P("wide", "tok"),
        P("tok"),
        P("tok", "wide"),
        P("tok", "wide"),
        P("wide", "tok"),
        P("var", None),
    )
    out_specs = (P("var"), P("var", "wide", "tok"))
    return jax.shard_map(
        per_device, mesh=mesh, in_specs=in_specs, out_specs=out_specs, check_vma=False
    )
```

```python
import functools
import math

import jax
import jax.numpy as jnp
from jax import lax
from jax.experimental import pallas as pl
from jax.experimental.pallas import tpu as pltpu
from jax.sharding import PartitionSpec as P

D = 8192
SIDE = 8


def block_groups():
    return [
        [(2 * a + i) * SIDE + 2 * b + j for i in range(2) for j in range(2)]
        for a in range(SIDE // 2)
        for b in range(SIDE // 2)
    ]


def stride_groups():
    return [
        [(2 * a + i) * SIDE + 2 * b + j for a in range(SIDE // 2) for b in range(SIDE // 2)]
        for i in range(2)
        for j in range(2)
    ]


VMEM = pl.BlockSpec(memory_space=pltpu.VMEM)
ANY = pl.BlockSpec(memory_space=pl.ANY)
COPIES = 8


def call(kernel, out_shape, in_specs, flops, size, scratch=(), out_spec=None):
    out_specs = jax.tree.map(lambda _: out_spec or VMEM, out_shape)
    return pl.pallas_call(
        kernel,
        out_shape=out_shape,
        in_specs=in_specs,
        out_specs=out_specs,
        scratch_shapes=list(scratch),
        compiler_params=pltpu.CompilerParams(vmem_limit_bytes=16 * 1024 * 1024),
        cost_estimate=pl.CostEstimate(flops=flops, bytes_accessed=size, transcendentals=0),
    )


def block_slot():
    wide = lax.axis_index("wide")
    return wide // SIDE % 2 * 2 + wide % 2


def repeat(piece, out_ref, held_ref, sems):
    count = held_ref.shape[0]
    for i in range(count):
        held_ref[i] = piece
    copies = [
        pltpu.make_async_copy(held_ref, out_ref.at[pl.ds(i * count, count)], sems.at[i])
        for i in range(COPIES)
    ]
    for copy in copies:
        copy.start()
    for copy in copies:
        copy.wait()


def repeated(kernel, out_shape, in_specs):
    count = out_shape.shape[0] // COPIES
    size = 4 * math.prod(out_shape.shape)
    scratch = [
        pltpu.VMEM((count,) + out_shape.shape[1:], out_shape.dtype),
        pltpu.SemaphoreType.DMA((COPIES,)),
    ]
    return call(kernel, out_shape, in_specs, 0, size, scratch, ANY)


def spread_kernel(tokens_ref, out_ref, held_ref, sems):
    width = out_ref.shape[2]
    tokens = tokens_ref[...].astype(jnp.float32)
    left, right = tokens[:, :width], tokens[:, width:]
    odd = lax.axis_index("wide") % 2 == 1
    first = jnp.where(odd, right, left)
    second = jnp.where(odd, left, right)
    upper = lax.broadcasted_iota(jnp.int32, first.shape, 0) < 4
    low = jnp.where(upper, first, pltpu.roll(second, 4, 0))
    high = jnp.where(upper, pltpu.roll(first, 4, 0), second)
    piece = jnp.where(lax.axis_index("var") == 0, low, high).astype(out_ref.dtype)
    repeat(piece, out_ref, held_ref, sems)


def parent_kernel(tokens_ref, gain_ref, weights_any, out_ref, rows_ref, weights_ref, sems):
    n_shards, _, width = tokens_ref.shape
    local = weights_ref.shape[1]
    copies = [
        pltpu.make_async_copy(weights_any.at[pl.ds(i * local, local)], weights_ref.at[i], sems.at[i]) for i in range(2)
    ]
    for copy in copies:
        copy.start()
    lanes = out_ref.shape[1] // 2
    step = 16
    squares = []
    for i in range(0, n_shards, step):
        part = tokens_ref[i : i + step].astype(jnp.float32).reshape(step // 2, 2, 8, width)
        even, odd = part[:, 0], part[:, 1]
        upper = lax.broadcasted_iota(jnp.int32, even.shape, 1) < 4
        left = jnp.where(upper, even, odd)
        right = jnp.where(upper, odd, even)
        rows = slice(i * 4, (i + step) * 4)
        left = left.reshape(step * 4, width)
        right = pltpu.roll(right, 4, 1).reshape(step * 4, width)
        squares.append(jnp.sum(left * left + right * right, axis=1, keepdims=True))
        rows_ref[rows, :width] = (left * gain_ref[:, :width]).astype(rows_ref.dtype)
        rows_ref[rows, width:] = (right * gain_ref[:, width:]).astype(rows_ref.dtype)
    squares = jnp.concatenate(squares, axis=0)
    hi = squares.astype(jnp.bfloat16).astype(jnp.float32)
    contract = (((1,), (1,)), ((), ()))
    copies[0].wait()
    gate = lax.dot_general(rows_ref[...], weights_ref[0], contract, preferred_element_type=jnp.float32)
    copies[1].wait()
    up = lax.dot_general(rows_ref[...], weights_ref[1], contract, preferred_element_type=jnp.float32)
    lane = lax.broadcasted_iota(jnp.int32, (squares.shape[0], lanes - local), 1)
    extra = jnp.where(lane == 0, hi, jnp.where(lane == 1, squares - hi, 0.0))
    out_ref[:, :local] = gate.astype(out_ref.dtype)
    out_ref[:, local:lanes] = extra.astype(out_ref.dtype)
    out_ref[:, lanes : lanes + local] = up.astype(out_ref.dtype)
    out_ref[:, lanes + local :] = jnp.zeros_like(extra).astype(out_ref.dtype)


def residual_kernel(own_ref, other_ref, drop_ref, down0, down1, down2, down3, out_ref):
    slot = block_slot()
    downs = (down0, down1, down2, down3)
    local = down0.shape[0]
    for half, hidden_ref in enumerate((own_ref, other_ref)):
        total = None
        for k in range(4):
            index = slot ^ k
            units = hidden_ref[index][:, :local] * drop_ref[index]
            term = jnp.dot(units, downs[k][...], preferred_element_type=jnp.float32)
            total = term if total is None else total + term
        out_ref[half] = (-total).astype(out_ref.dtype)


def select_kernel(names_ref, own_ref, other_ref, out_ref):
    rows = own_ref.shape[1]
    count = names_ref.shape[1]
    local = count
    for pair in range(2):
        names = names_ref[pair]
        for half, hidden_ref in enumerate((own_ref, other_ref)):
            total = None
            for i in range(2):
                units = lax.broadcasted_iota(jnp.int32, (count, local), 1) + i * local
                picker = jnp.where(units == names, 1.0, 0.0).astype(jnp.bfloat16)
                term = lax.dot_general(
                    picker,
                    hidden_ref[2 * pair + i][:, :local],
                    (((1,), (1,)), ((), ())),
                    preferred_element_type=jnp.float32,
                )
                total = term if total is None else total + term
            out_ref[pair, :, half * rows : (half + 1) * rows] = total.astype(out_ref.dtype)


def hidden_kernel(local, sums_ref, out_ref, held_ref, sems):
    total = sums_ref[0].astype(jnp.float32)
    for i in range(1, sums_ref.shape[0]):
        total = total + sums_ref[i].astype(jnp.float32)
    squares = total[:, local : local + 1] + total[:, local + 1 : local + 2]
    scale = lax.rsqrt(squares / D + 1e-05)
    half = total.shape[1] // 2
    gate = total[:, :half] * scale
    up = total[:, half:] * scale
    hidden = (gate / (1.0 + jnp.exp(-gate)) * up).astype(out_ref.dtype)
    repeat(hidden, out_ref, held_ref, sems)


def piece_kernel(shares_ref, out_ref, held_ref, sems):
    total = shares_ref[0].astype(jnp.float32)
    for i in range(1, shares_ref.shape[0]):
        total = total + shares_ref[i].astype(jnp.float32)
    repeat(total.astype(out_ref.dtype), out_ref, held_ref, sems)


def gradient_kernel(factor, chosen_ref, rounded_ref, out0, out1, out2, out3, error_ref, rows_ref):
    slot = block_slot()
    rounded = rounded_ref[...]
    block = out0.shape[0]
    for pair in range(2):
        product = jnp.dot(chosen_ref[pair], rounded, preferred_element_type=jnp.float32) * factor
        for i in range(2):
            rows_ref[2 * pair + i] = product[i * block : (i + 1) * block].astype(rows_ref.dtype)
    for k, out_ref in enumerate((out0, out1, out2, out3)):
        out_ref[...] = rows_ref[slot ^ k]
    errors = rounded.astype(jnp.float32)
    columns = jnp.sum((errors * errors).reshape(-1, 16, errors.shape[1]), axis=0)
    lanes = columns[:, :128]
    for i in range(1, columns.shape[1] // 128):
        lanes = lanes + columns[:, i * 128 : (i + 1) * 128]
    for i in range(error_ref.shape[0]):
        error_ref[i] = lanes


def interleave_kernel(in0, in1, in2, in3, out_ref):
    slot = block_slot()
    width = in0.shape[1]
    for k, in_ref in enumerate((in0, in1, in2, in3)):
        start = pl.multiple_of((slot ^ k) * width, 128)
        out_ref[:, pl.ds(start, width)] = in_ref[...]


def per_device(tokens, norm_gain, gate_parent, up_parent, down_parent, kept):
    n_wide = lax.axis_size("wide")
    n_tok = lax.axis_size("tok")
    core = lax.axis_index("var")
    wide = lax.axis_index("wide")
    row, col = wide // SIDE, wide % SIDE
    slot = (row % 2) * 2 + col % 2
    local = gate_parent.shape[1]
    width = tokens.shape[1]
    blocks = block_groups()

    half = tokens.shape[0] // 2
    pieces = repeated(
        spread_kernel,
        jax.ShapeDtypeStruct((n_wide, 2 * half, width // 2), jnp.bfloat16),
        [VMEM],
    )(tokens)
    gathered = lax.all_to_all(pieces, "wide", 0, 0)

    quarter = down_parent.shape[1] // 4
    downs = [lax.dynamic_slice_in_dim(down_parent, (slot ^ k) * quarter, quarter, 1) for k in range(4)]
    for k in range(1, 4):
        perm = [(w, w ^ ((k // 2) * SIDE + k % 2)) for w in range(n_wide)]
        downs[k] = lax.ppermute(downs[k], "wide", perm)

    weights = jnp.concatenate([gate_parent.T, up_parent.T], axis=0)
    gathered, weights = lax.optimization_barrier((gathered, weights))
    pad = (-local) % 128
    partial = call(
        parent_kernel,
        jax.ShapeDtypeStruct((n_wide * half, 2 * (local + pad)), jnp.bfloat16),
        [VMEM, VMEM, ANY],
        4 * n_wide * half * width * local,
        8 * width * local,
        [
            pltpu.VMEM((n_wide * half, width), jnp.bfloat16),
            pltpu.VMEM((2, local, width), jnp.bfloat16),
            pltpu.SemaphoreType.DMA((2,)),
        ],
    )(gathered, norm_gain.reshape(1, width), weights)
    rows = n_wide * half // n_tok

    scattered = lax.all_to_all(partial.reshape(n_tok, rows, 2 * (local + pad)), "tok", 0, 0)
    scattered, *downs = lax.optimization_barrier((scattered, *downs))
    hidden = repeated(
        functools.partial(hidden_kernel, local),
        jax.ShapeDtypeStruct((4 * n_tok, rows, local + pad), jnp.bfloat16),
        [VMEM],
    )(scattered)

    groups = [[t * n_wide + w for w in block for t in range(n_tok)] for block in blocks]
    hidden = lax.all_to_all(hidden, ("tok", "wide"), 0, 0, axis_index_groups=groups)
    hidden = hidden.reshape(4, n_tok * rows, local + pad)
    other = lax.ppermute(hidden, "var", [(0, 1), (1, 0)])
    total_rows = 2 * n_tok * rows

    var_kept = kept[0]
    block = var_kept.shape[0] // n_wide
    names = []
    drops = []
    for i in range(2):
        pair = (row // 2 * 2 + i) * (SIDE // 2) + col // 2
        name = lax.dynamic_slice_in_dim(var_kept, pair * 2 * block, 2 * block) - pair * 2 * local
        names.append(name)
        matches = jnp.arange(2 * local, dtype=jnp.int32)[:, None] == name[None, :]
        drops.append(jnp.where(jnp.any(matches, axis=1), 0.0, 1.0).astype(jnp.bfloat16))
    names = jnp.stack(names)[:, :, None]
    drop = jnp.concatenate(drops).reshape(4, 1, local)

    n_blocks = n_wide // 4
    product_flops = 2 * total_rows * 4 * local * quarter
    shares = call(
        residual_kernel,
        jax.ShapeDtypeStruct((2, total_rows // 2, quarter), jnp.bfloat16),
        [VMEM] * 7,
        product_flops,
        4 * total_rows * quarter,
    )(hidden, other, drop, *downs)
    shares = shares.reshape(n_blocks, total_rows // n_blocks, quarter)
    strides = stride_groups()
    shares = lax.all_to_all(shares, "wide", 0, 0, axis_index_groups=strides)
    pieces = repeated(piece_kernel, jax.ShapeDtypeStruct(shares.shape, jnp.bfloat16), [VMEM])(shares)
    rounded = lax.all_to_all(pieces, "wide", 0, 0, axis_index_groups=strides).reshape(total_rows, quarter)

    chosen = call(
        select_kernel,
        jax.ShapeDtypeStruct((2, 2 * block, total_rows), jnp.bfloat16),
        [VMEM] * 3,
        4 * total_rows * local * 4 * block,
        4 * total_rows * local,
    )(names, hidden, other)
    factor = 1.0 / math.sqrt(total_rows)
    *grads, errors = call(
        functools.partial(gradient_kernel, factor),
        (
            *[jax.ShapeDtypeStruct((block, quarter), jnp.bfloat16)] * 4,
            jax.ShapeDtypeStruct((4 * n_tok, 16, 128), jnp.float32),
        ),
        [VMEM, VMEM],
        2 * total_rows * 4 * block * quarter,
        4 * total_rows * quarter,
        [pltpu.VMEM((4, block, quarter), jnp.bfloat16)],
    )(chosen, rounded)
    errors = lax.all_to_all(errors, ("tok", "wide"), 0, 0, axis_index_groups=groups)
    loss = jnp.sum(errors) / (total_rows * D)
    for k in range(1, 4):
        perm = [(w, w ^ ((k // 2) * SIDE + k % 2)) for w in range(n_wide)]
        grads[k] = lax.ppermute(grads[k], "wide", perm)
    grad = call(
        interleave_kernel,
        jax.ShapeDtypeStruct((block, 4 * quarter), jnp.bfloat16),
        [VMEM] * 4,
        0,
        4 * block * quarter,
    )(*grads)
    return (loss.reshape(1), grad[None])


def solution(mesh):
    in_specs = (
        P("wide", "tok"),
        P("tok"),
        P("tok", "wide"),
        P("tok", "wide"),
        P("wide", "tok"),
        P("var", None),
    )
    out_specs = (P("var"), P("var", "wide", "tok"))
    return jax.shard_map(
        per_device, mesh=mesh, in_specs=in_specs, out_specs=out_specs, check_vma=False
    )
```

```python
import functools
import math

import jax
import jax.numpy as jnp
from jax import lax
from jax.experimental import pallas as pl
from jax.experimental.pallas import tpu as pltpu
from jax.sharding import PartitionSpec as P

D = 8192
SIDE = 8


def block_groups():
    return [
        [(2 * a + i) * SIDE + 2 * b + j for i in range(2) for j in range(2)]
        for a in range(SIDE // 2)
        for b in range(SIDE // 2)
    ]


def stride_groups():
    return [
        [(2 * a + i) * SIDE + 2 * b + j for a in range(SIDE // 2) for b in range(SIDE // 2)]
        for i in range(2)
        for j in range(2)
    ]


VMEM = pl.BlockSpec(memory_space=pltpu.VMEM)
ANY = pl.BlockSpec(memory_space=pl.ANY)
COPIES = 8


def call(kernel, out_shape, in_specs, flops, size, scratch=(), out_spec=None):
    out_specs = jax.tree.map(lambda _: out_spec or VMEM, out_shape)
    return pl.pallas_call(
        kernel,
        out_shape=out_shape,
        in_specs=in_specs,
        out_specs=out_specs,
        scratch_shapes=list(scratch),
        compiler_params=pltpu.CompilerParams(vmem_limit_bytes=16 * 1024 * 1024),
        cost_estimate=pl.CostEstimate(flops=flops, bytes_accessed=size, transcendentals=0),
    )


def block_slot():
    wide = lax.axis_index("wide")
    return wide // SIDE % 2 * 2 + wide % 2


def repeat(piece, out_ref, held_ref, sems):
    count = held_ref.shape[0]
    for i in range(count):
        held_ref[i] = piece
    copies = [
        pltpu.make_async_copy(held_ref, out_ref.at[pl.ds(i * count, count)], sems.at[i])
        for i in range(COPIES)
    ]
    for copy in copies:
        copy.start()
    for copy in copies:
        copy.wait()


def repeated(kernel, out_shape, in_specs):
    count = out_shape.shape[0] // COPIES
    size = 4 * math.prod(out_shape.shape)
    scratch = [
        pltpu.VMEM((count,) + out_shape.shape[1:], out_shape.dtype),
        pltpu.SemaphoreType.DMA((COPIES,)),
    ]
    return call(kernel, out_shape, in_specs, 0, size, scratch, ANY)


def spread_kernel(tokens_ref, out_ref, held_ref, sems):
    width = out_ref.shape[2]
    tokens = tokens_ref[...].astype(jnp.float32)
    left, right = tokens[:, :width], tokens[:, width:]
    odd = lax.axis_index("wide") % 2 == 1
    first = jnp.where(odd, right, left)
    second = jnp.where(odd, left, right)
    upper = lax.broadcasted_iota(jnp.int32, first.shape, 0) < 4
    low = jnp.where(upper, first, pltpu.roll(second, 4, 0))
    high = jnp.where(upper, pltpu.roll(first, 4, 0), second)
    piece = jnp.where(lax.axis_index("var") == 0, low, high).astype(out_ref.dtype)
    repeat(piece, out_ref, held_ref, sems)


def parent_kernel(tokens_ref, gain_ref, weights_ref, out_ref, rows_ref):
    n_shards, _, width = tokens_ref.shape
    local = weights_ref.shape[0] // 2
    lanes = out_ref.shape[1] // 2
    step = 16
    squares = []
    for i in range(0, n_shards, step):
        part = tokens_ref[i : i + step].astype(jnp.float32).reshape(step // 2, 2, 8, width)
        even, odd = part[:, 0], part[:, 1]
        upper = lax.broadcasted_iota(jnp.int32, even.shape, 1) < 4
        left = jnp.where(upper, even, odd)
        right = jnp.where(upper, odd, even)
        rows = slice(i * 4, (i + step) * 4)
        left = left.reshape(step * 4, width)
        right = pltpu.roll(right, 4, 1).reshape(step * 4, width)
        squares.append(jnp.sum(left * left + right * right, axis=1, keepdims=True))
        rows_ref[rows, :width] = (left * gain_ref[:, :width]).astype(rows_ref.dtype)
        rows_ref[rows, width:] = (right * gain_ref[:, width:]).astype(rows_ref.dtype)
    squares = jnp.concatenate(squares, axis=0)
    hi = squares.astype(jnp.bfloat16).astype(jnp.float32)
    contract = (((1,), (1,)), ((), ()))
    gate = lax.dot_general(rows_ref[...], weights_ref[:local], contract, preferred_element_type=jnp.float32)
    up = lax.dot_general(rows_ref[...], weights_ref[local:], contract, preferred_element_type=jnp.float32)
    lane = lax.broadcasted_iota(jnp.int32, (squares.shape[0], lanes - local), 1)
    extra = jnp.where(lane == 0, hi, jnp.where(lane == 1, squares - hi, 0.0))
    out_ref[:, :local] = gate.astype(out_ref.dtype)
    out_ref[:, local:lanes] = extra.astype(out_ref.dtype)
    out_ref[:, lanes : lanes + local] = up.astype(out_ref.dtype)
    out_ref[:, lanes + local :] = jnp.zeros_like(extra).astype(out_ref.dtype)


def residual_kernel(own_ref, other_ref, drop_ref, down0, down1, down2, down3, out_ref):
    slot = block_slot()
    downs = (down0, down1, down2, down3)
    local = down0.shape[0]
    for half, hidden_ref in enumerate((own_ref, other_ref)):
        total = None
        for k in range(4):
            index = slot ^ k
            units = hidden_ref[index][:, :local] * drop_ref[index]
            term = jnp.dot(units, downs[k][...], preferred_element_type=jnp.float32)
            total = term if total is None else total + term
        out_ref[half] = (-total).astype(out_ref.dtype)


def select_kernel(names_ref, own_ref, other_ref, out_ref):
    rows = own_ref.shape[1]
    count = names_ref.shape[1]
    local = count
    for pair in range(2):
        names = names_ref[pair]
        for half, hidden_ref in enumerate((own_ref, other_ref)):
            total = None
            for i in range(2):
                units = lax.broadcasted_iota(jnp.int32, (count, local), 1) + i * local
                picker = jnp.where(units == names, 1.0, 0.0).astype(jnp.bfloat16)
                term = lax.dot_general(
                    picker,
                    hidden_ref[2 * pair + i][:, :local],
                    (((1,), (1,)), ((), ())),
                    preferred_element_type=jnp.float32,
                )
                total = term if total is None else total + term
            out_ref[pair, :, half * rows : (half + 1) * rows] = total.astype(out_ref.dtype)


def hidden_kernel(local, sums_ref, out_ref, held_ref, sems):
    total = sums_ref[0].astype(jnp.float32)
    for i in range(1, sums_ref.shape[0]):
        total = total + sums_ref[i].astype(jnp.float32)
    squares = total[:, local : local + 1] + total[:, local + 1 : local + 2]
    scale = lax.rsqrt(squares / D + 1e-05)
    half = total.shape[1] // 2
    gate = total[:, :half] * scale
    up = total[:, half:] * scale
    hidden = (gate / (1.0 + jnp.exp(-gate)) * up).astype(out_ref.dtype)
    repeat(hidden, out_ref, held_ref, sems)


def piece_kernel(shares_ref, out_ref, held_ref, sems):
    total = shares_ref[0].astype(jnp.float32)
    for i in range(1, shares_ref.shape[0]):
        total = total + shares_ref[i].astype(jnp.float32)
    repeat(total.astype(out_ref.dtype), out_ref, held_ref, sems)


def gradient_kernel(factor, chosen_ref, rounded_ref, out0, out1, out2, out3, error_ref, rows_ref):
    slot = block_slot()
    rounded = rounded_ref[...]
    block = out0.shape[0]
    for pair in range(2):
        product = jnp.dot(chosen_ref[pair], rounded, preferred_element_type=jnp.float32) * factor
        for i in range(2):
            rows_ref[2 * pair + i] = product[i * block : (i + 1) * block].astype(rows_ref.dtype)
    for k, out_ref in enumerate((out0, out1, out2, out3)):
        out_ref[...] = rows_ref[slot ^ k]
    errors = rounded.astype(jnp.float32)
    columns = jnp.sum((errors * errors).reshape(-1, 16, errors.shape[1]), axis=0)
    lanes = columns[:, :128]
    for i in range(1, columns.shape[1] // 128):
        lanes = lanes + columns[:, i * 128 : (i + 1) * 128]
    for i in range(error_ref.shape[0]):
        error_ref[i] = lanes


def interleave_kernel(in0, in1, in2, in3, out_ref):
    slot = block_slot()
    width = in0.shape[1]
    for k, in_ref in enumerate((in0, in1, in2, in3)):
        start = pl.multiple_of((slot ^ k) * width, 128)
        out_ref[:, pl.ds(start, width)] = in_ref[...]


def per_device(tokens, norm_gain, gate_parent, up_parent, down_parent, kept):
    n_wide = lax.axis_size("wide")
    n_tok = lax.axis_size("tok")
    core = lax.axis_index("var")
    wide = lax.axis_index("wide")
    row, col = wide // SIDE, wide % SIDE
    slot = (row % 2) * 2 + col % 2
    local = gate_parent.shape[1]
    width = tokens.shape[1]
    blocks = block_groups()

    half = tokens.shape[0] // 2
    pieces = repeated(
        spread_kernel,
        jax.ShapeDtypeStruct((n_wide, 2 * half, width // 2), jnp.bfloat16),
        [VMEM],
    )(tokens)
    gathered = lax.all_to_all(pieces, "wide", 0, 0)

    quarter = down_parent.shape[1] // 4
    downs = [lax.dynamic_slice_in_dim(down_parent, (slot ^ k) * quarter, quarter, 1) for k in range(4)]
    for k in range(1, 4):
        perm = [(w, w ^ ((k // 2) * SIDE + k % 2)) for w in range(n_wide)]
        downs[k] = lax.ppermute(downs[k], "wide", perm)

    weights = jnp.concatenate([gate_parent.T, up_parent.T], axis=0)
    gathered, weights = lax.optimization_barrier((gathered, weights))
    pad = (-local) % 128
    partial = call(
        parent_kernel,
        jax.ShapeDtypeStruct((n_wide * half, 2 * (local + pad)), jnp.bfloat16),
        [VMEM] * 3,
        4 * n_wide * half * width * local,
        8 * width * local,
        [
            pltpu.VMEM((n_wide * half, width), jnp.bfloat16),
        ],
    )(gathered, norm_gain.reshape(1, width), weights)
    rows = n_wide * half // n_tok

    scattered = lax.all_to_all(partial.reshape(n_tok, rows, 2 * (local + pad)), "tok", 0, 0)
    scattered, *downs = lax.optimization_barrier((scattered, *downs))
    hidden = repeated(
        functools.partial(hidden_kernel, local),
        jax.ShapeDtypeStruct((4 * n_tok, rows, local + pad), jnp.bfloat16),
        [VMEM],
    )(scattered)

    groups = [[t * n_wide + w for w in block for t in range(n_tok)] for block in blocks]
    hidden = lax.all_to_all(hidden, ("tok", "wide"), 0, 0, axis_index_groups=groups)
    hidden = hidden.reshape(4, n_tok * rows, local + pad)
    other = lax.ppermute(hidden, "var", [(0, 1), (1, 0)])
    total_rows = 2 * n_tok * rows

    var_kept = kept[0]
    block = var_kept.shape[0] // n_wide
    names = []
    drops = []
    for i in range(2):
        pair = (row // 2 * 2 + i) * (SIDE // 2) + col // 2
        name = lax.dynamic_slice_in_dim(var_kept, pair * 2 * block, 2 * block) - pair * 2 * local
        names.append(name)
        matches = jnp.arange(2 * local, dtype=jnp.int32)[:, None] == name[None, :]
        drops.append(jnp.where(jnp.any(matches, axis=1), 0.0, 1.0).astype(jnp.bfloat16))
    names = jnp.stack(names)[:, :, None]
    drop = jnp.concatenate(drops).reshape(4, 1, local)

    n_blocks = n_wide // 4
    product_flops = 2 * total_rows * 4 * local * quarter
    shares = call(
        residual_kernel,
        jax.ShapeDtypeStruct((2, total_rows // 2, quarter), jnp.bfloat16),
        [VMEM] * 7,
        product_flops,
        4 * total_rows * quarter,
    )(hidden, other, drop, *downs)
    shares = shares.reshape(n_blocks, total_rows // n_blocks, quarter)
    strides = stride_groups()
    shares = lax.all_to_all(shares, "wide", 0, 0, axis_index_groups=strides)
    pieces = repeated(piece_kernel, jax.ShapeDtypeStruct(shares.shape, jnp.bfloat16), [VMEM])(shares)
    rounded = lax.all_to_all(pieces, "wide", 0, 0, axis_index_groups=strides).reshape(total_rows, quarter)

    chosen = call(
        select_kernel,
        jax.ShapeDtypeStruct((2, 2 * block, total_rows), jnp.bfloat16),
        [VMEM] * 3,
        4 * total_rows * local * 4 * block,
        4 * total_rows * local,
    )(names, hidden, other)
    factor = 1.0 / math.sqrt(total_rows)
    *grads, errors = call(
        functools.partial(gradient_kernel, factor),
        (
            *[jax.ShapeDtypeStruct((block, quarter), jnp.bfloat16)] * 4,
            jax.ShapeDtypeStruct((4 * n_tok, 16, 128), jnp.float32),
        ),
        [VMEM, VMEM],
        2 * total_rows * 4 * block * quarter,
        4 * total_rows * quarter,
        [pltpu.VMEM((4, block, quarter), jnp.bfloat16)],
    )(chosen, rounded)
    errors = lax.all_to_all(errors, ("tok", "wide"), 0, 0, axis_index_groups=groups)
    loss = jnp.sum(errors) / (total_rows * D)
    for k in range(1, 4):
        perm = [(w, w ^ ((k // 2) * SIDE + k % 2)) for w in range(n_wide)]
        grads[k] = lax.ppermute(grads[k], "wide", perm)
    grad = call(
        interleave_kernel,
        jax.ShapeDtypeStruct((block, 4 * quarter), jnp.bfloat16),
        [VMEM] * 4,
        0,
        4 * block * quarter,
    )(*grads)
    return (loss.reshape(1), grad[None])


def solution(mesh):
    in_specs = (
        P("wide", "tok"),
        P("tok"),
        P("tok", "wide"),
        P("tok", "wide"),
        P("wide", "tok"),
        P("var", None),
    )
    out_specs = (P("var"), P("var", "wide", "tok"))
    return jax.shard_map(
        per_device, mesh=mesh, in_specs=in_specs, out_specs=out_specs, check_vma=False
    )
```

```python
import functools
import math

import jax
import jax.numpy as jnp
from jax import lax
from jax.experimental import pallas as pl
from jax.experimental.pallas import tpu as pltpu
from jax.sharding import PartitionSpec as P

D = 8192
SIDE = 8


def block_groups():
    return [
        [(2 * a + i) * SIDE + 2 * b + j for i in range(2) for j in range(2)]
        for a in range(SIDE // 2)
        for b in range(SIDE // 2)
    ]


def stride_groups():
    return [
        [(2 * a + i) * SIDE + 2 * b + j for a in range(SIDE // 2) for b in range(SIDE // 2)]
        for i in range(2)
        for j in range(2)
    ]


VMEM = pl.BlockSpec(memory_space=pltpu.VMEM)


def call(kernel, out_shape, in_specs, flops, size, scratch=()):
    out_specs = jax.tree.map(lambda _: VMEM, out_shape)
    return pl.pallas_call(
        kernel,
        out_shape=out_shape,
        in_specs=in_specs,
        out_specs=out_specs,
        scratch_shapes=list(scratch),
        compiler_params=pltpu.CompilerParams(vmem_limit_bytes=16 * 1024 * 1024),
        cost_estimate=pl.CostEstimate(flops=flops, bytes_accessed=size, transcendentals=0),
    )


def block_slot():
    wide = lax.axis_index("wide")
    return wide // SIDE % 2 * 2 + wide % 2


def spread_kernel(tokens_ref, out_ref):
    width = out_ref.shape[2]
    tokens = tokens_ref[...].astype(jnp.float32)
    left, right = tokens[:, :width], tokens[:, width:]
    odd = lax.axis_index("wide") % 2 == 1
    first = jnp.where(odd, right, left)
    second = jnp.where(odd, left, right)
    upper = lax.broadcasted_iota(jnp.int32, first.shape, 0) < 4
    low = jnp.where(upper, first, pltpu.roll(second, 4, 0))
    high = jnp.where(upper, pltpu.roll(first, 4, 0), second)
    piece = jnp.where(lax.axis_index("var") == 0, low, high).astype(out_ref.dtype)
    for i in range(out_ref.shape[0]):
        out_ref[i] = piece


def parent_kernel(tokens_ref, gain_ref, weights_ref, out_ref, rows_ref):
    n_shards, _, width = tokens_ref.shape
    local = weights_ref.shape[0] // 2
    lanes = out_ref.shape[1] // 2
    step = 16
    squares = []
    for i in range(0, n_shards, step):
        part = tokens_ref[i : i + step].astype(jnp.float32).reshape(step // 2, 2, 8, width)
        even, odd = part[:, 0], part[:, 1]
        upper = lax.broadcasted_iota(jnp.int32, even.shape, 1) < 4
        left = jnp.where(upper, even, odd)
        right = jnp.where(upper, odd, even)
        rows = slice(i * 4, (i + step) * 4)
        left = left.reshape(step * 4, width)
        right = pltpu.roll(right, 4, 1).reshape(step * 4, width)
        squares.append(jnp.sum(left * left + right * right, axis=1, keepdims=True))
        rows_ref[rows, :width] = (left * gain_ref[:, :width]).astype(rows_ref.dtype)
        rows_ref[rows, width:] = (right * gain_ref[:, width:]).astype(rows_ref.dtype)
    squares = jnp.concatenate(squares, axis=0)
    hi = squares.astype(jnp.bfloat16).astype(jnp.float32)
    contract = (((1,), (1,)), ((), ()))
    gate = lax.dot_general(rows_ref[...], weights_ref[:local], contract, preferred_element_type=jnp.float32)
    up = lax.dot_general(rows_ref[...], weights_ref[local:], contract, preferred_element_type=jnp.float32)
    lane = lax.broadcasted_iota(jnp.int32, (squares.shape[0], lanes - local), 1)
    extra = jnp.where(lane == 0, hi, jnp.where(lane == 1, squares - hi, 0.0))
    out_ref[:, :local] = gate.astype(out_ref.dtype)
    out_ref[:, local:lanes] = extra.astype(out_ref.dtype)
    out_ref[:, lanes : lanes + local] = up.astype(out_ref.dtype)
    out_ref[:, lanes + local :] = jnp.zeros_like(extra).astype(out_ref.dtype)


def residual_kernel(own_ref, other_ref, drop_ref, down0, down1, down2, down3, out_ref):
    slot = block_slot()
    downs = (down0, down1, down2, down3)
    local = down0.shape[0]
    for half, hidden_ref in enumerate((own_ref, other_ref)):
        total = None
        for k in range(4):
            index = slot ^ k
            units = hidden_ref[index][:, :local] * drop_ref[index]
            term = jnp.dot(units, downs[k][...], preferred_element_type=jnp.float32)
            total = term if total is None else total + term
        out_ref[half] = (-total).astype(out_ref.dtype)


def select_kernel(names_ref, own_ref, other_ref, out_ref):
    rows = own_ref.shape[1]
    count = names_ref.shape[1]
    local = count
    for pair in range(2):
        names = names_ref[pair]
        for half, hidden_ref in enumerate((own_ref, other_ref)):
            total = None
            for i in range(2):
                units = lax.broadcasted_iota(jnp.int32, (count, local), 1) + i * local
                picker = jnp.where(units == names, 1.0, 0.0).astype(jnp.bfloat16)
                term = lax.dot_general(
                    picker,
                    hidden_ref[2 * pair + i][:, :local],
                    (((1,), (1,)), ((), ())),
                    preferred_element_type=jnp.float32,
                )
                total = term if total is None else total + term
            out_ref[pair, :, half * rows : (half + 1) * rows] = total.astype(out_ref.dtype)


def hidden_kernel(local, sums_ref, out_ref):
    total = sums_ref[0].astype(jnp.float32)
    for i in range(1, sums_ref.shape[0]):
        total = total + sums_ref[i].astype(jnp.float32)
    squares = total[:, local : local + 1] + total[:, local + 1 : local + 2]
    scale = lax.rsqrt(squares / D + 1e-05)
    half = total.shape[1] // 2
    gate = total[:, :half] * scale
    up = total[:, half:] * scale
    hidden = (gate / (1.0 + jnp.exp(-gate)) * up).astype(out_ref.dtype)
    for i in range(out_ref.shape[0]):
        out_ref[i] = hidden


def piece_kernel(shares_ref, out_ref):
    total = shares_ref[0].astype(jnp.float32)
    for i in range(1, shares_ref.shape[0]):
        total = total + shares_ref[i].astype(jnp.float32)
    piece = total.astype(out_ref.dtype)
    for i in range(out_ref.shape[0]):
        out_ref[i] = piece


def gradient_kernel(factor, chosen_ref, rounded_ref, out0, out1, out2, out3, error_ref, rows_ref):
    slot = block_slot()
    rounded = rounded_ref[...]
    block = out0.shape[0]
    for pair in range(2):
        product = jnp.dot(chosen_ref[pair], rounded, preferred_element_type=jnp.float32) * factor
        for i in range(2):
            rows_ref[2 * pair + i] = product[i * block : (i + 1) * block].astype(rows_ref.dtype)
    for k, out_ref in enumerate((out0, out1, out2, out3)):
        out_ref[...] = rows_ref[slot ^ k]
    errors = rounded.astype(jnp.float32)
    columns = jnp.sum(errors * errors, axis=0, keepdims=True)
    lanes = columns[:, :128]
    for i in range(1, columns.shape[1] // 128):
        lanes = lanes + columns[:, i * 128 : (i + 1) * 128]
    line = lax.broadcasted_iota(jnp.int32, (8, 128), 0)
    lanes = jnp.where(line == 0, lanes, 0.0)
    for i in range(error_ref.shape[0]):
        error_ref[i] = lanes


def interleave_kernel(in0, in1, in2, in3, out_ref):
    slot = block_slot()
    width = in0.shape[1]
    for k, in_ref in enumerate((in0, in1, in2, in3)):
        start = pl.multiple_of((slot ^ k) * width, 128)
        out_ref[:, pl.ds(start, width)] = in_ref[...]


def per_device(tokens, norm_gain, gate_parent, up_parent, down_parent, kept):
    n_wide = lax.axis_size("wide")
    n_tok = lax.axis_size("tok")
    wide = lax.axis_index("wide")
    row, col = wide // SIDE, wide % SIDE
    slot = (row % 2) * 2 + col % 2
    local = gate_parent.shape[1]
    width = tokens.shape[1]
    blocks = block_groups()

    half = tokens.shape[0] // 2
    pieces = call(
        spread_kernel,
        jax.ShapeDtypeStruct((n_wide, 2 * half, width // 2), jnp.bfloat16),
        [VMEM],
        0,
        2 * n_wide * half * width,
    )(tokens)
    gathered = lax.all_to_all(pieces, "wide", 0, 0)

    quarter = down_parent.shape[1] // 4
    downs = [lax.dynamic_slice_in_dim(down_parent, (slot ^ k) * quarter, quarter, 1) for k in range(4)]
    for k in range(1, 4):
        perm = [(w, w ^ ((k // 2) * SIDE + k % 2)) for w in range(n_wide)]
        downs[k] = lax.ppermute(downs[k], "wide", perm)

    weights = jnp.concatenate([gate_parent.T, up_parent.T], axis=0)
    gathered, weights = lax.optimization_barrier((gathered, weights))
    pad = (-local) % 128
    partial = call(
        parent_kernel,
        jax.ShapeDtypeStruct((n_wide * half, 2 * (local + pad)), jnp.bfloat16),
        [VMEM] * 3,
        4 * n_wide * half * width * local,
        8 * width * local,
        [pltpu.VMEM((n_wide * half, width), jnp.bfloat16)],
    )(gathered, norm_gain.reshape(1, width), weights)
    rows = n_wide * half // n_tok

    scattered = lax.all_to_all(partial.reshape(n_tok, rows, 2 * (local + pad)), "tok", 0, 0)
    scattered, *downs = lax.optimization_barrier((scattered, *downs))
    hidden = call(
        functools.partial(hidden_kernel, local),
        jax.ShapeDtypeStruct((4 * n_tok, rows, local + pad), jnp.bfloat16),
        [VMEM],
        0,
        16 * rows * local,
    )(scattered)

    groups = [[t * n_wide + w for w in block for t in range(n_tok)] for block in blocks]
    hidden = lax.all_to_all(hidden, ("tok", "wide"), 0, 0, axis_index_groups=groups)
    hidden = hidden.reshape(4, n_tok * rows, local + pad)
    other = lax.ppermute(hidden, "var", [(0, 1), (1, 0)])
    total_rows = 2 * n_tok * rows

    var_kept = kept[0]
    block = var_kept.shape[0] // n_wide
    names = []
    drops = []
    for i in range(2):
        pair = (row // 2 * 2 + i) * (SIDE // 2) + col // 2
        name = lax.dynamic_slice_in_dim(var_kept, pair * 2 * block, 2 * block) - pair * 2 * local
        names.append(name)
        matches = jnp.arange(2 * local, dtype=jnp.int32)[:, None] == name[None, :]
        drops.append(jnp.where(jnp.any(matches, axis=1), 0.0, 1.0).astype(jnp.bfloat16))
    names = jnp.stack(names)[:, :, None]
    drop = jnp.concatenate(drops).reshape(4, 1, local)

    n_blocks = n_wide // 4
    product_flops = 2 * total_rows * 4 * local * quarter
    shares = call(
        residual_kernel,
        jax.ShapeDtypeStruct((2, total_rows // 2, quarter), jnp.bfloat16),
        [VMEM] * 7,
        product_flops,
        4 * total_rows * quarter,
    )(hidden, other, drop, *downs)
    shares = shares.reshape(n_blocks, total_rows // n_blocks, quarter)
    strides = stride_groups()
    shares = lax.all_to_all(shares, "wide", 0, 0, axis_index_groups=strides)
    pieces = call(piece_kernel, jax.ShapeDtypeStruct(shares.shape, jnp.bfloat16), [VMEM], 0, 4 * total_rows * quarter)(shares)
    rounded = lax.all_to_all(pieces, "wide", 0, 0, axis_index_groups=strides).reshape(total_rows, quarter)

    chosen = call(
        select_kernel,
        jax.ShapeDtypeStruct((2, 2 * block, total_rows), jnp.bfloat16),
        [VMEM] * 3,
        4 * total_rows * local * 4 * block,
        4 * total_rows * local,
    )(names, hidden, other)
    factor = 1.0 / math.sqrt(total_rows)
    *grads, errors = call(
        functools.partial(gradient_kernel, factor),
        (
            *[jax.ShapeDtypeStruct((block, quarter), jnp.bfloat16)] * 4,
            jax.ShapeDtypeStruct((4 * n_tok, 8, 128), jnp.float32),
        ),
        [VMEM, VMEM],
        2 * total_rows * 4 * block * quarter,
        4 * total_rows * quarter,
        [pltpu.VMEM((4, block, quarter), jnp.bfloat16)],
    )(chosen, rounded)
    errors = lax.all_to_all(errors, ("tok", "wide"), 0, 0, axis_index_groups=groups)
    loss = jnp.sum(errors) / (total_rows * D)
    for k in range(1, 4):
        perm = [(w, w ^ ((k // 2) * SIDE + k % 2)) for w in range(n_wide)]
        grads[k] = lax.ppermute(grads[k], "wide", perm)
    grad = call(
        interleave_kernel,
        jax.ShapeDtypeStruct((block, 4 * quarter), jnp.bfloat16),
        [VMEM] * 4,
        0,
        4 * block * quarter,
    )(*grads)
    return (loss.reshape(1), grad[None])


def solution(mesh):
    in_specs = (
        P("wide", "tok"),
        P("tok"),
        P("tok", "wide"),
        P("tok", "wide"),
        P("wide", "tok"),
        P("var", None),
    )
    out_specs = (P("var"), P("var", "wide", "tok"))
    return jax.shard_map(
        per_device, mesh=mesh, in_specs=in_specs, out_specs=out_specs, check_vma=False
    )
```
